32 devices in a mesh: cuts: 4 (over x, core), tile: 8 (over z, y).
Axes of the slice: x: 2, y: 2, z: 4, core: 2. Of those that a mesh axis runs over, the one named last changes fastest.
Arguments:
- acquired: bfloat16 [524288, 256], P(('cuts', 'tile')), may hold values from -6 to 6
- stencil: bfloat16 [2048, 1024], P('tile'), may hold values from -0.0390625 to 0.0390625
- send_slots: int32 [32, 8, 1280], P(('cuts', 'tile')), may hold values from 0 to 16383
- send_lines: int32 [32, 8, 1280], P(('cuts', 'tile')), may hold values from 0 to 1023
- send_counts: int32 [32, 8], P(('cuts', 'tile')), may hold values from 1 to 1280, as said below
- return_slots: int32 [32, 8, 128], P(('cuts', 'tile')), may hold values from 0 to 255
- return_counts: int32 [32, 8], P(('cuts', 'tile')), may hold values from 1 to 128, as said below
Outputs:
- field_out: bfloat16 [32, 256, 256], P(('cuts', 'tile'))
- returned: bfloat16 [256, 128, 256], P(('cuts', 'tile'))
The draws below stay inside these ranges and needn't reach their ends.
Inputs may be any that keep to these rules, and one draw needn't show every extreme that they name: `send_counts`: some tile receives 1280 rows from every device. `return_counts`: some reader tile receives 128 lines from every owner.
All inputs are finite; a program needn't handle non-finite values.
Results may differ from the reference program's by a relative error of at most 0.00075.
Values may be sent and summed in bfloat16 or wider, within the bound.
A program may use at most 192 MiB of HBM per device.

```python
import jax
import jax.numpy as jnp
from jax import lax

NX = 256
NY = 256
TAPS = 4
ITERS = 2
ZDEV = 1
ROWS_DEV = 16384
CAP = 1280
RCAP = 128
NZ = 32
ACQ = 524288
N_CUTS = 4
N_TILE = 8


def skewed_counts(key, rows_total, cols_total, most):
    rank = jax.random.permutation(jax.random.fold_in(key, 11), cols_total)
    high = jnp.where(rank % 4 == 0, most, most // (1 + rank % 4)) + 1
    low = max(1, most // 8)
    drawn = jax.random.randint(jax.random.fold_in(key, 12), (rows_total, cols_total), low, high[None, :])
    return jnp.where(rank[None, :] == 0, most, drawn).astype(jnp.int32)


def draw_send_counts(key, part):
    return skewed_counts(key, N_CUTS * N_TILE, N_TILE, CAP)


def draw_return_counts(key, part):
    return skewed_counts(jax.random.fold_in(key, 5), N_CUTS * N_TILE, N_TILE, RCAP)


def plant(result, stream_key, low, top_value):
    spot = [jax.random.randint(jax.random.fold_in(stream_key, axis), (), 0, length) for axis, length in enumerate(result.shape)]
    main_axis = result.shape.index(max(result.shape))
    beside = spot[:main_axis] + [(spot[main_axis] + 1) % result.shape[main_axis]] + spot[main_axis + 1:]
    return result.at[tuple(spot)].set(low).at[tuple(beside)].set(top_value)


def level_of(own_key, dims, cuts, smallest, high):
    gain, own = 1.0, jax.random.fold_in(own_key, 6)
    for dim, shards_of in cuts:
        steps = jnp.exp(jax.random.uniform(jax.random.fold_in(own, dim), (shards_of,), jnp.float32, smallest / len(cuts), high / len(cuts)))
        gain = gain * jnp.repeat(steps, dims[dim] // shards_of).reshape([-1 if axis == dim else 1 for axis in range(len(dims))])
    return gain


def centred(stream_key, extent, width, limit, cuts=(), held_as=jnp.bfloat16):
    array = width * jax.random.normal(stream_key, extent, jnp.float32)
    if cuts:
        array = array * level_of(stream_key, extent, cuts, -0.22, 0.18)
    return jnp.clip(array, -limit, limit).astype(held_as)


def setup_inputs(seed: int = 0) -> dict:
    key_list = jax.random.split(jax.random.key(seed), 8)
    acquired = centred(key_list[0], (ACQ, NX), 1.0, 6.0, ((0, 32),))
    stencil = centred(key_list[1], (N_TILE * NX, TAPS * NX), (NX * N_TILE * CAP * 2 // (ZDEV * NY)) ** -0.5, 0.0390625, ((0, 8),))
    send_slots = plant(jax.random.randint(key_list[2], (N_CUTS * N_TILE, N_TILE, CAP), 0, ROWS_DEV), jax.random.fold_in(key_list[2], 1), 0, ROWS_DEV - 1).astype(jnp.int32)
    send_lines = plant(jax.random.randint(key_list[3], (N_CUTS * N_TILE, N_TILE, CAP), 0, N_CUTS * ZDEV * NY), jax.random.fold_in(key_list[3], 1), 0, (N_CUTS * ZDEV * NY) - 1).astype(jnp.int32)
    send_counts = draw_send_counts(jax.random.fold_in(key_list[7], 71), 0)
    return_slots = plant(jax.random.randint(key_list[5], (N_CUTS * N_TILE, N_TILE, RCAP), 0, ZDEV * NY), jax.random.fold_in(key_list[5], 1), 0, (ZDEV * NY) - 1).astype(jnp.int32)
    return_counts = draw_return_counts(jax.random.fold_in(key_list[7], 71), 0)
    return dict(acquired=acquired, stencil=stencil, send_slots=send_slots, send_lines=send_lines, send_counts=send_counts, return_slots=return_slots, return_counts=return_counts)


def neighbour_sum(inner):
    zpad = jnp.pad(inner, ((1, 1), (0, 0), (0, 0)))
    ypad = jnp.pad(inner, ((0, 0), (1, 1), (0, 0)))
    xpad = jnp.pad(inner, ((0, 0), (0, 0), (1, 1)))
    return zpad[2:] + zpad[:-2] + ypad[:, 2:] + ypad[:, :-2] + xpad[:, :, 2:] + xpad[:, :, :-2]


def reference(acquired, stencil, send_slots, send_lines, send_counts, return_slots, return_counts):
    devices_all = N_CUTS * N_TILE
    rows_all = acquired.reshape(devices_all, ROWS_DEV, NX)
    stencils = stencil.reshape(N_TILE, NX, TAPS * NX).astype(jnp.float32)
    slot_index = jnp.arange(CAP, dtype=jnp.int32)
    tap_offsets = jnp.arange(TAPS, dtype=jnp.int32)
    tile_ids = jnp.arange(N_TILE, dtype=jnp.int32)

    def add_source(raw_field, source_item):
        src_rows, slots, line_ids, counts = source_item
        usable = slot_index[None, :] < counts[:, None]
        picked = src_rows[slots]
        picked = jnp.where(usable[:, :, None], picked, jnp.zeros_like(picked)).astype(jnp.float32)
        terms = jnp.einsum("tcr,trk->tck", picked, stencils, precision=lax.Precision.HIGHEST)
        cut_ids = line_ids // (ZDEV * NY)
        plane_ids = (line_ids // NY) % ZDEV
        row_in_plane = line_ids % NY
        depth = (cut_ids * N_TILE + tile_ids[:, None]) * ZDEV + plane_ids
        target = depth[:, :, None] * NY + (row_in_plane[:, :, None] + tap_offsets) % NY
        raw_field = raw_field.at[target.reshape(-1)].add(terms.reshape(-1, NX))
        return raw_field, None

    raw_field = jnp.zeros((NZ * NY, NX), jnp.float32)
    raw_field, _ = lax.scan(add_source, raw_field, (rows_all, send_slots, send_lines, send_counts))
    smooth_field = raw_field.reshape(NZ, NY, NX)
    for sweep in range(ITERS):
        smooth_field = smooth_field + 0.15 * (neighbour_sum(smooth_field) - 6.0 * smooth_field)
    field_out = smooth_field.astype(jnp.bfloat16)
    per_device = field_out.reshape(devices_all, ZDEV * NY, NX)
    fetched = jax.vmap(lambda dev_field, read_ids: dev_field[read_ids])(per_device, return_slots)
    read_index = jnp.arange(RCAP, dtype=jnp.int32)
    usable_back = read_index[None, None, :] < return_counts[:, :, None]
    fetched = jnp.where(usable_back[..., None], fetched, jnp.zeros_like(fetched))
    returned = fetched.reshape(N_CUTS, N_TILE, N_TILE, RCAP, NX).transpose(0, 2, 1, 3, 4)
    returned = returned.reshape(devices_all * N_TILE, RCAP, NX)
    return field_out, returned
```

```python
import functools

import jax
import jax.numpy as jnp
from jax import lax
from jax.experimental import pallas as pl
from jax.experimental.pallas import tpu as pltpu
from jax.sharding import PartitionSpec as P

NX = 256
NY = 256
TAPS = 4
ITERS = 2
ZDEV = 1
LOAD_ROWS = 1024
UNROLL = 8


def line_sum_kernel(slots, lines, counts, acquired, out, rows, staged, even, odd, load_sem):
    tile = pl.program_id(0)
    loads = acquired.shape[0] // LOAD_ROWS

    def load(step):
        return pltpu.make_async_copy(
            acquired.at[pl.ds(pl.multiple_of(step * LOAD_ROWS, LOAD_ROWS), LOAD_ROWS)],
            staged.at[step],
            load_sem.at[step],
        )

    @pl.when(tile == 0)
    def _():
        @pl.loop(0, loads)
        def _(step):
            load(step).start()

        @pl.loop(0, loads)
        def _(step):
            load(step).wait()
            rows[pl.ds(pl.multiple_of(step * LOAD_ROWS, LOAD_ROWS), LOAD_ROWS), :] = staged[
                step
            ].astype(jnp.float32)

    even[...] = jnp.zeros_like(even)
    odd[...] = jnp.zeros_like(odd)
    count = counts[0, tile]

    def add(j, total):
        line = lines[0, tile, j]
        total[pl.ds(line, 1), :] += rows[pl.ds(slots[0, tile, j], 1), :]

    groups = count // UNROLL

    @pl.loop(0, groups)
    def _(group):
        for u in range(UNROLL):
            add(group * UNROLL + u, (even, odd)[u % 2])

    @pl.loop(groups * UNROLL, count)
    def _(j):
        add(j, even)

    cores, others = out.shape[0], out.shape[1]
    for core in range(cores):
        for x in range(others):
            span = pl.ds((x * cores + core) * NY, NY)
            out[core, x, 0] = even[span, :] + odd[span, :]


def line_sums(acquired, slots, lines, counts, cut_count):
    tile_count = slots.shape[1]
    cores = 2
    rows_dev = acquired.shape[0]
    loads = rows_dev // LOAD_ROWS
    group_lines = cut_count * NY
    return pl.pallas_call(
        line_sum_kernel,
        grid=(tile_count,),
        out_shape=jax.ShapeDtypeStruct((cores, cut_count // cores, tile_count, NY, NX), jnp.float32),
        in_specs=[
            pl.BlockSpec(memory_space=pltpu.SMEM),
            pl.BlockSpec(memory_space=pltpu.SMEM),
            pl.BlockSpec(memory_space=pltpu.SMEM),
            pl.BlockSpec(memory_space=pl.ANY),
        ],
        out_specs=pl.BlockSpec(
            (cores, cut_count // cores, 1, NY, NX), lambda t: (0, 0, t, 0, 0)
        ),
        scratch_shapes=[
            pltpu.VMEM((rows_dev, NX), jnp.float32),
            pltpu.VMEM((loads, LOAD_ROWS, NX), jnp.bfloat16),
            pltpu.VMEM((group_lines, NX), jnp.float32),
            pltpu.VMEM((group_lines, NX), jnp.float32),
            pltpu.SemaphoreType.DMA((loads,)),
        ],
        compiler_params=pltpu.CompilerParams(vmem_limit_bytes=48 * 1024 * 1024),
        name="line_sums",
    )(slots, lines, counts, acquired)


def with_halo(cells, sides, width):
    for axis, dim in sides:
        count = lax.axis_size(axis)
        ends = count - 1
        head = lax.slice_in_dim(cells, 0, width, axis=dim)
        tail = lax.slice_in_dim(cells, cells.shape[dim] - width, cells.shape[dim], axis=dim)
        cells = jnp.concatenate(
            [
                lax.ppermute(tail, axis, [(i, (i + 1) % count) for i in range(ends)]),
                cells,
                lax.ppermute(head, axis, [((i + 1) % count, i) for i in range(ends)]),
            ],
            axis=dim,
        )
    return cells


def local_sum(padded, inner):
    ypad = jnp.pad(inner, ((0, 0), (1, 1), (0, 0)))
    xpad = jnp.pad(inner, ((0, 0), (0, 0), (1, 1)))
    return padded[2:] + padded[:-2] + ypad[:, 2:] + ypad[:, :-2] + xpad[:, :, 2:] + xpad[:, :, :-2]


def apply_stencil(line_field, stencil):
    plane_total = line_field.shape[0] // NY
    product = jnp.dot(line_field, stencil.astype(jnp.float32), precision=lax.Precision.HIGHEST)
    product = product.reshape(plane_total, NY, TAPS, NX)
    accum_planes = product[:, :, 0, :]
    for shift_k in range(1, TAPS):
        accum_planes = accum_planes + jnp.roll(product[:, :, shift_k, :], shift_k, axis=1)
    return accum_planes


def local(acquired, stencil, send_slots, send_lines, send_counts, return_slots, return_counts):
    tile_count = lax.axis_size("tile")
    cut_count = lax.axis_size("cuts")
    sums = line_sums(acquired, send_slots, send_lines, send_counts, cut_count)
    sums = sums.transpose(1, 0, 2, 3, 4).reshape(cut_count * tile_count, NY, NX)
    own_lines = lax.psum_scatter(sums, ("cuts", "tile"), scatter_dimension=0, tiled=True)
    smooth_field = apply_stencil(own_lines.reshape(ZDEV * NY, NX), stencil)
    for sweep in range(ITERS):
        padded = with_halo(smooth_field, ((("cuts", "tile"), 0),), 1)
        smooth_field = smooth_field + 0.15 * (local_sum(padded, smooth_field) - 6.0 * smooth_field)
    field_out = smooth_field.astype(jnp.bfloat16)
    read_ids = return_slots[0]
    read_counts = return_counts[0]
    read_total = read_ids.shape[1]
    flat_field = field_out.reshape(ZDEV * NY, NX)
    read_index = jnp.arange(read_total, dtype=jnp.int32)
    usable_back = read_index[None, :] < read_counts[:, None]
    own_range = jnp.arange(ZDEV * NY, dtype=jnp.int32)
    selector = (read_ids.reshape(-1)[:, None] == own_range[None, :]) & usable_back.reshape(-1)[
        :, None
    ]
    outgoing = jnp.dot(
        selector.astype(jnp.bfloat16), flat_field, preferred_element_type=jnp.float32
    )
    outgoing = outgoing.astype(jnp.bfloat16).reshape(tile_count, read_total, NX)
    returned = lax.all_to_all(outgoing, "tile", split_axis=0, concat_axis=0, tiled=True)
    return (field_out, returned)


def solution(mesh):
    in_specs = (
        P(("cuts", "tile"), None),
        P("tile", None),
        P(("cuts", "tile"), None, None),
        P(("cuts", "tile"), None, None),
        P(("cuts", "tile"), None),
        P(("cuts", "tile"), None, None),
        P(("cuts", "tile"), None),
    )
    out_specs = (P(("cuts", "tile"), None, None), P(("cuts", "tile"), None, None))
    return jax.shard_map(local, mesh=mesh, in_specs=in_specs, out_specs=out_specs, check_vma=False)
```

```python
import jax
import jax.numpy as jnp
from jax import lax
from jax.experimental import pallas as pl
from jax.experimental.pallas import tpu as pltpu
from jax.sharding import PartitionSpec as P

NX = 256
NY = 256
TAPS = 4
ZDEV = 1
LOAD_ROWS = 1024
UNROLL = 8
LEVELS = 32767.0
WEIGHT = 0.15


def line_sum_kernel(slots, lines, counts, acquired, out, rows, staged, even, odd, load_sem):
    tile = pl.program_id(0)
    loads = acquired.shape[0] // LOAD_ROWS

    def load(step):
        return pltpu.make_async_copy(
            acquired.at[pl.ds(pl.multiple_of(step * LOAD_ROWS, LOAD_ROWS), LOAD_ROWS)],
            staged.at[step],
            load_sem.at[step],
        )

    @pl.when(tile == 0)
    def _():
        @pl.loop(0, loads)
        def _(step):
            load(step).start()

        @pl.loop(0, loads)
        def _(step):
            load(step).wait()
            rows[pl.ds(pl.multiple_of(step * LOAD_ROWS, LOAD_ROWS), LOAD_ROWS), :] = staged[
                step
            ].astype(jnp.float32)

    even[...] = jnp.zeros_like(even)
    odd[...] = jnp.zeros_like(odd)
    count = counts[0, tile]

    def add(j, total):
        line = lines[0, tile, j]
        total[pl.ds(line, 1), :] += rows[pl.ds(slots[0, tile, j], 1), :]

    groups = count // UNROLL

    @pl.loop(0, groups)
    def _(group):
        for u in range(UNROLL):
            add(group * UNROLL + u, (even, odd)[u % 2])

    @pl.loop(groups * UNROLL, count)
    def _(j):
        add(j, even)

    cores, others = out.shape[0], out.shape[1]
    for core in range(cores):
        for x in range(others):
            span = pl.ds((x * cores + core) * NY, NY)
            out[core, x, 0] = even[span, :] + odd[span, :]


def line_sums(acquired, slots, lines, counts, cut_count):
    tile_count = slots.shape[1]
    cores = 2
    rows_dev = acquired.shape[0]
    loads = rows_dev // LOAD_ROWS
    group_lines = cut_count * NY
    return pl.pallas_call(
        line_sum_kernel,
        grid=(tile_count,),
        out_shape=jax.ShapeDtypeStruct((cores, cut_count // cores, tile_count, NY, NX), jnp.float32),
        in_specs=[
            pl.BlockSpec(memory_space=pltpu.SMEM),
            pl.BlockSpec(memory_space=pltpu.SMEM),
            pl.BlockSpec(memory_space=pltpu.SMEM),
            pl.BlockSpec(memory_space=pl.ANY),
        ],
        out_specs=pl.BlockSpec(
            (cores, cut_count // cores, 1, NY, NX), lambda t: (0, 0, t, 0, 0)
        ),
        scratch_shapes=[
            pltpu.VMEM((rows_dev, NX), jnp.float32),
            pltpu.VMEM((loads, LOAD_ROWS, NX), jnp.bfloat16),
            pltpu.VMEM((group_lines, NX), jnp.float32),
            pltpu.VMEM((group_lines, NX), jnp.float32),
            pltpu.SemaphoreType.DMA((loads,)),
        ],
        compiler_params=pltpu.CompilerParams(vmem_limit_bytes=48 * 1024 * 1024),
        name="line_sums",
    )(slots, lines, counts, acquired)


def code(plane):
    most = jnp.max(jnp.abs(plane), axis=0, keepdims=True)
    most = jnp.maximum(most, 1e-30)
    coded = jnp.round(plane * (LEVELS / most)).astype(jnp.int32).astype(jnp.int16)
    return coded, jnp.broadcast_to(most * (1.0 / LEVELS), (8, NX))


def decode(coded, scale):
    return coded.astype(jnp.int32).astype(jnp.float32) * scale[0:1, :]


def shifted(plane, by, axis):
    zeros = jnp.zeros((abs(by), NX) if axis == 0 else (NY, abs(by)), plane.dtype)
    size = plane.shape[axis]
    if by > 0:
        return jnp.concatenate([zeros, lax.slice_in_dim(plane, 0, size - by, axis=axis)], axis)
    return jnp.concatenate([lax.slice_in_dim(plane, -by, size, axis=axis), zeros], axis)


def in_plane(plane):
    around = shifted(plane, 1, 0) + shifted(plane, -1, 0)
    around += shifted(plane, 1, 1) + shifted(plane, -1, 1)
    return (1.0 - 6.0 * WEIGHT) * plane + WEIGHT * around


def field_kernel(
    partial, stencil, selector, field_out, returned,
    own, core_in, q1_out, q1_in, s1_out, s1_in, q2_out, q2_in, s2_out, s2_in,
    q3_out, q3_in, s3_out, s3_in, q4_out, q4_in, s4_out, s4_in, back_out,
    own_sem, core_send, core_recv, send1, recv1, send2, recv2, send3, recv3,
    send4, recv4, send5, recv5,
):
    tiles = partial.shape[2]
    side = partial.shape[1]
    depth = tiles // side
    half = depth // 2
    spread = half * side
    cut, tile = lax.axis_index("cuts"), lax.axis_index("tile")
    x, core = cut // 2, cut % 2
    z, y = tile // side, tile % side
    me = cut * tiles + tile
    last = 2 * side * tiles - 1

    def at(x_to, y_to, z_to):
        return (x_to * 2 + core, z_to * side + y_to)

    def remote(src, dst, send, recv, device):
        return pltpu.make_async_remote_copy(
            src_ref=src, dst_ref=dst, send_sem=send, recv_sem=recv,
            device_id=device, device_id_type=pl.DeviceIdType.MESH,
        )

    partner = (x * 2 + 1 - core, tile)
    barrier = pltpu.get_barrier_semaphore()

    def greet(device):
        pl.semaphore_signal(
            barrier, inc=1, device_id=device, device_id_type=pl.DeviceIdType.MESH
        )

    greet(partner)
    for r in range(1, side):
        greet(at((x + r) % side, y, z))
    for s in range(1, tiles):
        greet((cut, (tile + s) % tiles))
    reach = (-2, -1, 1, 2)
    there = [(me + step >= 0) & (me + step <= last) for step in reach]
    for step, exists in zip(reach, there):
        @pl.when(exists)
        def _():
            greet(((me + step) // tiles, (me + step) % tiles))
    met = 1 + side - 1 + tiles - 1
    for exists in there:
        met = met + jnp.where(exists, 1, 0)
    pl.semaphore_wait(barrier, met)

    def place(r, group, i):
        o, h = i // half, i % half
        if group == 0:
            return (x + r) % side, h * side + (y + 1 + o) % side
        return (x + 1 + o) % side, (half + h) * side + (y + r) % side

    def core_copy(r, group, i):
        x_to, t_to = place(r, group, i)
        return remote(
            partial.at[1 - core, x_to, t_to], core_in.at[r - 1, group, i],
            core_send.at[r - 1, group, i], core_recv.at[r - 1, group, i], partner,
        )

    def own_copy(r, group, i):
        x_to, t_to = place(r, group, i)
        return pltpu.make_async_copy(
            partial.at[core, x_to, t_to], own.at[r - 1, group, i], own_sem.at[r - 1, group, i]
        )

    @pl.loop(0, side * spread)
    def _(n):
        r, i = n // spread + 1, n % spread
        for group in range(2):
            core_copy(r, group, i).start()
            own_copy(r, group, i).start()

    def pair(q_out, q_in, s_out, s_in, send, recv, at_out, at_in, device):
        return (
            remote(q_out.at[at_out], q_in.at[at_in], send.at[(0, *at_in)], recv.at[(0, *at_in)], device),
            remote(s_out.at[at_out], s_in.at[at_in], send.at[(1, *at_in)], recv.at[(1, *at_in)], device),
        )

    def copies1(r, group, i):
        device = at((x + r) % side, y, z) if group == 0 else at(x, (y + r) % side, z)
        slot = (r - 1, group, i)
        return pair(q1_out, q1_in, s1_out, s1_in, send1, recv1, slot, slot, device)

    def copies2(group, o, h):
        r = o + 1
        device = at(x, (y + r) % side, z) if group == 0 else at((x + r) % side, y, z)
        slot = (group, o, h)
        return pair(q2_out, q2_in, s2_out, s2_in, send2, recv2, slot, slot, device)

    def copies3(s):
        slot = (s - 1,)
        return pair(
            q3_out, q3_in, s3_out, s3_in, send3, recv3, slot, slot, at(x, y, (z + s) % depth)
        )

    def chip_sum(r, group, i):
        core_copy(r, group, i).wait_recv()
        own_copy(r, group, i).wait()
        return own[r - 1, group, i] + core_in[r - 1, group, i]

    @pl.loop(0, (side - 1) * spread)
    def _(n):
        r, i = n // spread + 1, n % spread
        for group in range(2):
            q1_out[r - 1, group, i], s1_out[r - 1, group, i] = code(chip_sum(r, group, i))
            for copy in copies1(r, group, i):
                copy.start()

    def kept(group, i):
        total = chip_sum(side, group, i)
        for r in range(1, side):
            for copy in copies1(r, group, i):
                copy.wait_recv()
            total += decode(q1_in[r - 1, group, i], s1_in[r - 1, group, i])
        return total

    @pl.loop(0, (side - 1) * half)
    def _(i):
        o, h = i // half, i % half
        for group in range(2):
            q2_out[group, o, h], s2_out[group, o, h] = code(kept(group, i))
            for copy in copies2(group, o, h):
                copy.start()

    @pl.loop(0, half)
    def _(h):
        i = (side - 1) * half + h
        for group in range(2):
            own[side - 1, group, i] = kept(group, i)

    def column(z_to):
        group, h = z_to // half, z_to % half
        total = own[side - 1, group, (side - 1) * half + h]
        for o in range(side - 1):
            total += decode(q2_in[group, o, h], s2_in[group, o, h])
        return total

    @pl.loop(0, (side - 1) * half)
    def _(i):
        for group in range(2):
            for copy in copies2(group, i // half, i % half):
                copy.wait_recv()

    @pl.loop(1, depth)
    def _(s):
        q3_out[s - 1], s3_out[s - 1] = code(column((z + s) % depth))
        for copy in copies3(s):
            copy.start()

    lines = column(z)
    for s in range(1, depth):
        for copy in copies3(s):
            copy.wait_recv()
        lines += decode(q3_in[s - 1], s3_in[s - 1])

    weights = stencil[...]
    raw = jnp.zeros((NY, NX), jnp.float32)
    rest = lines
    product = jnp.zeros((NY, TAPS * NX), jnp.float32)
    for _ in range(3):
        part = rest.astype(jnp.bfloat16)
        rest = rest - part.astype(jnp.float32)
        product += jnp.dot(part, weights, preferred_element_type=jnp.float32)
    raw = product[:, :NX]
    for k in range(1, TAPS):
        term = product[:, k * NX : (k + 1) * NX]
        raw += jnp.concatenate([term[NY - k :], term[: NY - k]], axis=0)

    q4_out[...], s4_out[...] = code(raw)

    def copies4(n):
        to = me + reach[n]
        device = (to // tiles, to % tiles)
        return (
            remote(q4_out, q4_in.at[n], send4.at[0, n], recv4.at[0, n], device),
            remote(s4_out, s4_in.at[n], send4.at[1, n], recv4.at[1, n], device),
        )

    for n in range(4):
        @pl.when(there[n])
        def _():
            for copy in copies4(n):
                copy.start()

    for n in range(4):
        from_there = there[3 - n]

        @pl.when(from_there)
        def _():
            for copy in copies4(n):
                copy.wait_recv()

        @pl.when(jnp.logical_not(from_there))
        def _():
            q4_in[n] = jnp.zeros((NY, NX), jnp.int16)
            s4_in[n] = jnp.zeros((8, NX), jnp.float32)

    near = decode(q4_in[1], s4_in[1]) + decode(q4_in[2], s4_in[2])
    far = decode(q4_in[0], s4_in[0]) + decode(q4_in[3], s4_in[3])
    beside = jnp.where(there[1], 1.0, 0.0) + jnp.where(there[2], 1.0, 0.0)
    once = in_plane(raw) + (2.0 * WEIGHT) * near
    smooth = in_plane(once) + (WEIGHT * WEIGHT) * (far + beside * raw)
    field = smooth.astype(jnp.bfloat16)
    field_out[0] = field

    reads = returned.shape[1]

    def back(t2):
        chosen = selector[pl.ds(pl.multiple_of(t2 * reads, reads), reads), :]
        return jnp.dot(chosen, field_out[0], preferred_element_type=jnp.float32).astype(jnp.bfloat16)

    def copy5(s):
        return remote(
            back_out.at[s - 1], returned.at[tile], send5.at[s - 1], recv5.at[s - 1],
            (cut, (tile + s) % tiles),
        )

    @pl.loop(1, tiles)
    def _(s):
        back_out[s - 1] = back((tile + s) % tiles)
        copy5(s).start()

    returned[tile] = back(tile)

    @pl.loop(0, side * spread)
    def _(n):
        for group in range(2):
            core_copy(n // spread + 1, group, n % spread).wait_send()

    @pl.loop(0, (side - 1) * spread)
    def _(n):
        for group in range(2):
            for copy in copies1(n // spread + 1, group, n % spread):
                copy.wait_send()

    @pl.loop(0, (side - 1) * half)
    def _(i):
        for group in range(2):
            for copy in copies2(group, i // half, i % half):
                copy.wait_send()

    @pl.loop(1, depth)
    def _(s):
        for copy in copies3(s):
            copy.wait_send()

    for n in range(4):
        @pl.when(there[n])
        def _():
            for copy in copies4(n):
                copy.wait_send()

    @pl.loop(1, tiles)
    def _(s):
        copy5(s).wait_send()
        source = (tile - s + tiles) % tiles
        remote(
            back_out.at[s - 1], returned.at[source], send5.at[s - 1], recv5.at[s - 1],
            (cut, (tile + s) % tiles),
        ).wait_recv()


def finish(partial, stencil, selector, reads):
    side, tiles = partial.shape[1], partial.shape[2]
    depth = tiles // side
    half = depth // 2
    spread = half * side
    dma = pltpu.SemaphoreType.DMA

    def coded(*lead):
        return [
            pltpu.VMEM((*lead, NY, NX), jnp.int16),
            pltpu.VMEM((*lead, NY, NX), jnp.int16),
            pltpu.VMEM((*lead, 8, NX), jnp.float32),
            pltpu.VMEM((*lead, 8, NX), jnp.float32),
        ]

    vmem = pl.BlockSpec(memory_space=pltpu.VMEM)
    return pl.pallas_call(
        field_kernel,
        out_shape=(
            jax.ShapeDtypeStruct((1, NY, NX), jnp.bfloat16),
            jax.ShapeDtypeStruct((tiles, reads, NX), jnp.bfloat16),
        ),
        in_specs=[pl.BlockSpec(memory_space=pl.ANY), vmem, vmem],
        out_specs=(vmem, vmem),
        scratch_shapes=[
            pltpu.VMEM((side, 2, spread, NY, NX), jnp.float32),
            pltpu.VMEM((side, 2, spread, NY, NX), jnp.float32),
            *coded(side - 1, 2, spread),
            *coded(2, side - 1, half),
            *coded(depth - 1),
            pltpu.VMEM((NY, NX), jnp.int16),
            pltpu.VMEM((4, NY, NX), jnp.int16),
            pltpu.VMEM((8, NX), jnp.float32),
            pltpu.VMEM((4, 8, NX), jnp.float32),
            pltpu.VMEM((tiles - 1, reads, NX), jnp.bfloat16),
            dma((side, 2, spread)),
            dma((side, 2, spread)),
            dma((side, 2, spread)),
            dma((2, side - 1, 2, spread)),
            dma((2, side - 1, 2, spread)),
            dma((2, 2, side - 1, half)),
            dma((2, 2, side - 1, half)),
            dma((2, depth - 1)),
            dma((2, depth - 1)),
            dma((2, 4)),
            dma((2, 4)),
            dma((tiles - 1,)),
            dma((tiles - 1,)),
        ],
        compiler_params=pltpu.CompilerParams(
            collective_id=0, has_side_effects=True, vmem_limit_bytes=60 * 1024 * 1024
        ),
        name="reduce_smooth_return",
    )(partial, stencil, selector)


def local(acquired, stencil, send_slots, send_lines, send_counts, return_slots, return_counts):
    cut_count = lax.axis_size("cuts")
    sums = line_sums(acquired, send_slots, send_lines, send_counts, cut_count)
    read_ids, read_counts = return_slots[0], return_counts[0]
    reads = read_ids.shape[1]
    usable = jnp.arange(reads, dtype=jnp.int32)[None, :] < read_counts[:, None]
    wanted = jnp.where(usable, read_ids, -1).reshape(-1)
    selector = (wanted[:, None] == jnp.arange(ZDEV * NY, dtype=jnp.int32)[None, :]).astype(
        jnp.bfloat16
    )
    return finish(sums, stencil, selector, reads)


def solution(mesh):
    in_specs = (
        P(("cuts", "tile"), None),
        P("tile", None),
        P(("cuts", "tile"), None, None),
        P(("cuts", "tile"), None, None),
        P(("cuts", "tile"), None),
        P(("cuts", "tile"), None, None),
        P(("cuts", "tile"), None),
    )
    out_specs = (P(("cuts", "tile"), None, None), P(("cuts", "tile"), None, None))
    return jax.shard_map(local, mesh=mesh, in_specs=in_specs, out_specs=out_specs, check_vma=False)
```

```python
import jax
import jax.numpy as jnp
from jax import lax
from jax.experimental import pallas as pl
from jax.experimental.pallas import tpu as pltpu
from jax.sharding import PartitionSpec as P

NX = 256
NY = 256
TAPS = 4
ZDEV = 1
LOAD_ROWS = 1024
UNROLL = 8
LEVELS = 32767.0
WEIGHT = 0.15
GROUPS = 8
GROUP = NY // GROUPS


def code(plane):
    coded, scales = [], []
    for g in range(GROUPS):
        block = plane[g * GROUP : (g + 1) * GROUP]
        most = jnp.maximum(jnp.max(jnp.abs(block), axis=0, keepdims=True), 1e-30)
        coded.append(jnp.round(block * (LEVELS / most)).astype(jnp.int32).astype(jnp.int16))
        scales.append(most * (1.0 / LEVELS))
    return jnp.concatenate(coded, axis=0), jnp.concatenate(scales, axis=0)


def decode(coded, scale):
    parts = []
    for g in range(GROUPS):
        part = coded[g * GROUP : (g + 1) * GROUP].astype(jnp.int32).astype(jnp.float32)
        parts.append(part * scale[g : g + 1])
    return jnp.concatenate(parts, axis=0)


def line_sum_kernel(
    slots_in, lines_in, counts, acquired, kept_out, sent_out, scale_out,
    rows, staged, even, odd, slots, lines, load_sem, index_sem,
):
    tile = pl.program_id(0)
    loads = acquired.shape[0] // LOAD_ROWS

    def load(step):
        return pltpu.make_async_copy(
            acquired.at[pl.ds(pl.multiple_of(step * LOAD_ROWS, LOAD_ROWS), LOAD_ROWS)],
            staged.at[step],
            load_sem.at[step],
        )

    index_copies = (
        pltpu.make_async_copy(slots_in.at[0], slots, index_sem.at[0]),
        pltpu.make_async_copy(lines_in.at[0], lines, index_sem.at[1]),
    )

    @pl.when(tile == 0)
    def _():
        for copy in index_copies:
            copy.start()

        @pl.loop(0, loads)
        def _(step):
            load(step).start()

        @pl.loop(0, loads)
        def _(step):
            load(step).wait()
            rows[pl.ds(pl.multiple_of(step * LOAD_ROWS, LOAD_ROWS), LOAD_ROWS), :] = staged[
                step
            ].astype(jnp.float32)

        for copy in index_copies:
            copy.wait()

    even[...] = jnp.zeros_like(even)
    odd[...] = jnp.zeros_like(odd)
    count = counts[0, tile]
    groups = count // UNROLL

    @pl.loop(0, groups)
    def _(group):
        first = group * UNROLL
        spots = [pl.ds(lines[tile, first + u], 1) for u in range(UNROLL)]
        added = [rows[pl.ds(slots[tile, first + u], 1), :] for u in range(UNROLL)]
        for q in range(0, UNROLL, 4):
            held = [(even, even, odd, odd)[u][spots[q + u], :] for u in range(4)]
            for p in (0, 2):
                total = (even, odd)[p // 2]
                same = jnp.where(spots[q + p].start == spots[q + p + 1].start, 1.0, 0.0)
                total[spots[q + p], :] = held[p] + added[q + p]
                total[spots[q + p + 1], :] = held[p + 1] + (added[q + p + 1] + same * added[q + p])

    @pl.loop(groups * UNROLL, count)
    def _(j):
        even[pl.ds(lines[tile, j], 1), :] += rows[pl.ds(slots[tile, j], 1), :]

    core = lax.axis_index("cuts") % 2
    for x in range(kept_out.shape[0]):
        span = pl.ds(pl.multiple_of((x * 2 + core) * NY, NY), NY)
        kept_out[x, 0] = even[span, :] + odd[span, :]
        span = pl.ds(pl.multiple_of((x * 2 + 1 - core) * NY, NY), NY)
        sent_out[x, 0], scale_out[x, 0] = code(even[span, :] + odd[span, :])


def line_sums(acquired, slots, lines, counts, cut_count):
    tile_count = slots.shape[1]
    side = cut_count // 2
    rows_dev = acquired.shape[0]
    loads = rows_dev // LOAD_ROWS
    group_lines = cut_count * NY
    hbm = pl.BlockSpec(memory_space=pl.ANY)
    return pl.pallas_call(
        line_sum_kernel,
        grid=(tile_count,),
        out_shape=(
            jax.ShapeDtypeStruct((side, tile_count, NY, NX), jnp.float32),
            jax.ShapeDtypeStruct((side, tile_count, NY, NX), jnp.int16),
            jax.ShapeDtypeStruct((side, tile_count, GROUPS, NX), jnp.float32),
        ),
        in_specs=[hbm, hbm, pl.BlockSpec(memory_space=pltpu.SMEM), hbm],
        out_specs=(
            pl.BlockSpec((side, 1, NY, NX), lambda t: (0, t, 0, 0)),
            pl.BlockSpec((side, 1, NY, NX), lambda t: (0, t, 0, 0)),
            pl.BlockSpec((side, 1, GROUPS, NX), lambda t: (0, t, 0, 0)),
        ),
        scratch_shapes=[
            pltpu.VMEM((rows_dev, NX), jnp.float32),
            pltpu.VMEM((loads, LOAD_ROWS, NX), jnp.bfloat16),
            pltpu.VMEM((group_lines, NX), jnp.float32),
            pltpu.VMEM((group_lines, NX), jnp.float32),
            pltpu.SMEM(slots.shape[1:], jnp.int32),
            pltpu.SMEM(lines.shape[1:], jnp.int32),
            pltpu.SemaphoreType.DMA((loads,)),
            pltpu.SemaphoreType.DMA((2,)),
        ],
        compiler_params=pltpu.CompilerParams(vmem_limit_bytes=48 * 1024 * 1024),
        name="line_sums",
    )(slots, lines, counts, acquired)


def shifted(plane, by, axis):
    zeros = jnp.zeros((abs(by), NX) if axis == 0 else (NY, abs(by)), plane.dtype)
    size = plane.shape[axis]
    if by > 0:
        return jnp.concatenate([zeros, lax.slice_in_dim(plane, 0, size - by, axis=axis)], axis)
    return jnp.concatenate([lax.slice_in_dim(plane, -by, size, axis=axis), zeros], axis)


def in_plane(plane):
    around = shifted(plane, 1, 0) + shifted(plane, -1, 0)
    around += shifted(plane, 1, 1) + shifted(plane, -1, 1)
    return (1.0 - 6.0 * WEIGHT) * plane + WEIGHT * around


def field_kernel(
    kept_sums, sent_sums, sent_scales, stencil, read_ids, read_counts, field_out, returned,
    own, core_in, core_scale, chosen, q1_out, q1_in, s1_out, s1_in, q2_out, q2_in, s2_out, s2_in,
    q3_out, q3_in, s3_out, s3_in, q4_out, q4_in, s4_out, s4_in, back_out,
    own_sem, core_send, core_recv, send1, recv1, send2, recv2, send3, recv3,
    send4, recv4, send5, recv5,
):
    side, tiles = kept_sums.shape[:2]
    depth = tiles // side
    half = depth // 2
    spread = half * side
    cut, tile = lax.axis_index("cuts"), lax.axis_index("tile")
    x, core = cut // 2, cut % 2
    z, y = tile // side, tile % side
    me = cut * tiles + tile
    last = 2 * side * tiles - 1

    def at(x_to, y_to, z_to):
        return (x_to * 2 + core, z_to * side + y_to)

    def remote(src, dst, send, recv, device):
        return pltpu.make_async_remote_copy(
            src_ref=src, dst_ref=dst, send_sem=send, recv_sem=recv,
            device_id=device, device_id_type=pl.DeviceIdType.MESH,
        )

    partner = (x * 2 + 1 - core, tile)
    barrier = pltpu.get_barrier_semaphore()

    def greet(device):
        pl.semaphore_signal(
            barrier, inc=1, device_id=device, device_id_type=pl.DeviceIdType.MESH
        )

    greet(partner)
    for r in range(1, side):
        greet(at((x + r) % side, y, z))
    for s in range(1, tiles):
        greet((cut, (tile + s) % tiles))
    reach = (-2, -1, 1, 2)
    there = [(me + step >= 0) & (me + step <= last) for step in reach]
    for step, exists in zip(reach, there):
        @pl.when(exists)
        def _():
            greet(((me + step) // tiles, (me + step) % tiles))
    met = 1 + side - 1 + tiles - 1
    for exists in there:
        met = met + jnp.where(exists, 1, 0)
    pl.semaphore_wait(barrier, met)

    def place(r, group, i):
        h, o = i // side, i % side
        if group == 0:
            return (x + r) % side, h * side + (y + 1 + o) % side
        return (x + 1 + o) % side, (half + h) * side + (y + r) % side

    def core_copies(r, group, i):
        x_to, t_to = place(r, group, i)
        slot = (r - 1, group, i)
        return (
            remote(
                sent_sums.at[x_to, t_to], core_in.at[slot],
                core_send.at[(0, *slot)], core_recv.at[(0, *slot)], partner,
            ),
            remote(
                sent_scales.at[x_to, t_to], core_scale.at[slot],
                core_send.at[(1, *slot)], core_recv.at[(1, *slot)], partner,
            ),
        )

    def own_copy(r, group, i):
        x_to, t_to = place(r, group, i)
        return pltpu.make_async_copy(
            kept_sums.at[x_to, t_to], own.at[r - 1, group, i], own_sem.at[r - 1, group, i]
        )

    @pl.loop(0, side * spread)
    def _(n):
        r, i = n // spread + 1, n % spread
        for group in range(2):
            for copy in core_copies(r, group, i):
                copy.start()
            own_copy(r, group, i).start()

    reads = returned.shape[1]
    field_lines = lax.broadcasted_iota(jnp.int32, (NY, reads), 0)
    read_index = lax.broadcasted_iota(jnp.int32, (1, reads), 1)
    for t2 in range(tiles):
        wanted = jnp.where(read_index < read_counts[0, t2], read_ids[0, t2 : t2 + 1, :], -1)
        chosen[t2] = jnp.where(field_lines == wanted, 1.0, 0.0).astype(jnp.bfloat16)

    def pair(q_out, q_in, s_out, s_in, send, recv, at_out, at_in, device):
        return (
            remote(q_out.at[at_out], q_in.at[at_in], send.at[(0, *at_in)], recv.at[(0, *at_in)], device),
            remote(s_out.at[at_out], s_in.at[at_in], send.at[(1, *at_in)], recv.at[(1, *at_in)], device),
        )

    def copies1(r, group, i):
        device = at((x + r) % side, y, z) if group == 0 else at(x, (y + r) % side, z)
        slot = (r - 1, group, i)
        return pair(q1_out, q1_in, s1_out, s1_in, send1, recv1, slot, slot, device)

    def copies2(group, o, h):
        r = o + 1
        device = at(x, (y + r) % side, z) if group == 0 else at((x + r) % side, y, z)
        slot = (group, o, h)
        return pair(q2_out, q2_in, s2_out, s2_in, send2, recv2, slot, slot, device)

    def copies3(s):
        slot = (s - 1,)
        return pair(
            q3_out, q3_in, s3_out, s3_in, send3, recv3, slot, slot, at(x, y, (z + s) % depth)
        )

    def chip_sum(r, group, i):
        for copy in core_copies(r, group, i):
            copy.wait_recv()
        own_copy(r, group, i).wait()
        return own[r - 1, group, i] + decode(core_in[r - 1, group, i], core_scale[r - 1, group, i])

    @pl.loop(0, (side - 1) * spread)
    def _(n):
        r, i = n // spread + 1, n % spread
        for group in range(2):
            q1_out[r - 1, group, i], s1_out[r - 1, group, i] = code(chip_sum(r, group, i))
            for copy in copies1(r, group, i):
                copy.start()

    def kept(group, i):
        total = chip_sum(side, group, i)
        for r in range(1, side):
            for copy in copies1(r, group, i):
                copy.wait_recv()
            total += decode(q1_in[r - 1, group, i], s1_in[r - 1, group, i])
        return total

    @pl.loop(0, half)
    def _(h):
        for o in range(side - 1):
            for group in range(2):
                q2_out[group, o, h], s2_out[group, o, h] = code(kept(group, h * side + o))
                for copy in copies2(group, o, h):
                    copy.start()
        for group in range(2):
            i = h * side + side - 1
            own[side - 1, group, i] = kept(group, i)

    def column(z_to):
        group, h = z_to // half, z_to % half
        total = own[side - 1, group, h * side + side - 1]
        for o in range(side - 1):
            total += decode(q2_in[group, o, h], s2_in[group, o, h])
        return total

    def column_of(h, group):
        for o in range(side - 1):
            for copy in copies2(group, o, h):
                copy.wait_recv()
        z_to = group * half + h
        s = (z_to - z + depth) % depth

        @pl.when(s > 0)
        def _():
            q3_out[s - 1], s3_out[s - 1] = code(column(z_to))
            for copy in copies3(s):
                copy.start()

    @pl.loop(0, half)
    def _(h):
        for group in range(2):
            column_of(h, group)

    lines = column(z)
    for s in range(1, depth):
        for copy in copies3(s):
            copy.wait_recv()
        lines += decode(q3_in[s - 1], s3_in[s - 1])

    weights = stencil[...]
    raw = jnp.zeros((NY, NX), jnp.float32)
    rest = lines
    product = jnp.zeros((NY, TAPS * NX), jnp.float32)
    for _ in range(3):
        part = rest.astype(jnp.bfloat16)
        rest = rest - part.astype(jnp.float32)
        product += jnp.dot(part, weights, preferred_element_type=jnp.float32)
    raw = product[:, :NX]
    for k in range(1, TAPS):
        term = product[:, k * NX : (k + 1) * NX]
        raw += jnp.concatenate([term[NY - k :], term[: NY - k]], axis=0)

    q4_out[...], s4_out[...] = code(raw)

    def copies4(n):
        to = me + reach[n]
        device = (to // tiles, to % tiles)
        return (
            remote(q4_out, q4_in.at[n], send4.at[0, n], recv4.at[0, n], device),
            remote(s4_out, s4_in.at[n], send4.at[1, n], recv4.at[1, n], device),
        )

    for n in range(4):
        @pl.when(there[n])
        def _():
            for copy in copies4(n):
                copy.start()

    for n in range(4):
        from_there = there[3 - n]

        @pl.when(from_there)
        def _():
            for copy in copies4(n):
                copy.wait_recv()

        @pl.when(jnp.logical_not(from_there))
        def _():
            q4_in[n] = jnp.zeros((NY, NX), jnp.int16)
            s4_in[n] = jnp.zeros((GROUPS, NX), jnp.float32)

    near = decode(q4_in[1], s4_in[1]) + decode(q4_in[2], s4_in[2])
    far = decode(q4_in[0], s4_in[0]) + decode(q4_in[3], s4_in[3])
    beside = jnp.where(there[1], 1.0, 0.0) + jnp.where(there[2], 1.0, 0.0)
    once = in_plane(raw) + (2.0 * WEIGHT) * near
    smooth = in_plane(once) + (WEIGHT * WEIGHT) * (far + beside * raw)
    field = smooth.astype(jnp.bfloat16)
    field_out[0] = field

    def back(t2):
        return lax.dot_general(
            chosen[t2], field_out[0], (((0,), (0,)), ((), ())), preferred_element_type=jnp.float32
        ).astype(jnp.bfloat16)

    def copy5(s):
        return remote(
            back_out.at[s - 1], returned.at[tile], send5.at[s - 1], recv5.at[s - 1],
            (cut, (tile + s) % tiles),
        )

    @pl.loop(1, tiles)
    def _(s):
        back_out[s - 1] = back((tile + s) % tiles)
        copy5(s).start()

    returned[tile] = back(tile)

    @pl.loop(0, side * spread)
    def _(n):
        for group in range(2):
            for copy in core_copies(n // spread + 1, group, n % spread):
                copy.wait_send()

    @pl.loop(0, (side - 1) * spread)
    def _(n):
        for group in range(2):
            for copy in copies1(n // spread + 1, group, n % spread):
                copy.wait_send()

    @pl.loop(0, (side - 1) * half)
    def _(i):
        for group in range(2):
            for copy in copies2(group, i // half, i % half):
                copy.wait_send()

    @pl.loop(1, depth)
    def _(s):
        for copy in copies3(s):
            copy.wait_send()

    for n in range(4):
        @pl.when(there[n])
        def _():
            for copy in copies4(n):
                copy.wait_send()

    @pl.loop(1, tiles)
    def _(s):
        copy5(s).wait_send()
        source = (tile - s + tiles) % tiles
        remote(
            back_out.at[s - 1], returned.at[source], send5.at[s - 1], recv5.at[s - 1],
            (cut, (tile + s) % tiles),
        ).wait_recv()


def finish(sums, stencil, read_ids, read_counts):
    side, tiles = sums[0].shape[:2]
    reads = read_ids.shape[2]
    depth = tiles // side
    half = depth // 2
    spread = half * side
    dma = pltpu.SemaphoreType.DMA

    def coded(*lead):
        return [
            pltpu.VMEM((*lead, NY, NX), jnp.int16),
            pltpu.VMEM((*lead, NY, NX), jnp.int16),
            pltpu.VMEM((*lead, GROUPS, NX), jnp.float32),
            pltpu.VMEM((*lead, GROUPS, NX), jnp.float32),
        ]

    vmem = pl.BlockSpec(memory_space=pltpu.VMEM)
    hbm = pl.BlockSpec(memory_space=pl.ANY)
    return pl.pallas_call(
        field_kernel,
        out_shape=(
            jax.ShapeDtypeStruct((1, NY, NX), jnp.bfloat16),
            jax.ShapeDtypeStruct((tiles, reads, NX), jnp.bfloat16),
        ),
        in_specs=[hbm, hbm, hbm, vmem, vmem, pl.BlockSpec(memory_space=pltpu.SMEM)],
        out_specs=(vmem, vmem),
        scratch_shapes=[
            pltpu.VMEM((side, 2, spread, NY, NX), jnp.float32),
            pltpu.VMEM((side, 2, spread, NY, NX), jnp.int16),
            pltpu.VMEM((side, 2, spread, GROUPS, NX), jnp.float32),
            pltpu.VMEM((tiles, NY, reads), jnp.bfloat16),
            *coded(side - 1, 2, spread),
            *coded(2, side - 1, half),
            *coded(depth - 1),
            pltpu.VMEM((NY, NX), jnp.int16),
            pltpu.VMEM((4, NY, NX), jnp.int16),
            pltpu.VMEM((GROUPS, NX), jnp.float32),
            pltpu.VMEM((4, GROUPS, NX), jnp.float32),
            pltpu.VMEM((tiles - 1, reads, NX), jnp.bfloat16),
            dma((side, 2, spread)),
            dma((2, side, 2, spread)),
            dma((2, side, 2, spread)),
            dma((2, side - 1, 2, spread)),
            dma((2, side - 1, 2, spread)),
            dma((2, 2, side - 1, half)),
            dma((2, 2, side - 1, half)),
            dma((2, depth - 1)),
            dma((2, depth - 1)),
            dma((2, 4)),
            dma((2, 4)),
            dma((tiles - 1,)),
            dma((tiles - 1,)),
        ],
        compiler_params=pltpu.CompilerParams(
            collective_id=0, has_side_effects=True, vmem_limit_bytes=60 * 1024 * 1024
        ),
        name="reduce_smooth_return",
    )(*sums, stencil, read_ids, read_counts)


def local(acquired, stencil, send_slots, send_lines, send_counts, return_slots, return_counts):
    cut_count = lax.axis_size("cuts")
    sums = line_sums(acquired, send_slots, send_lines, send_counts, cut_count)
    return finish(sums, stencil, return_slots, return_counts)


def solution(mesh):
    in_specs = (
        P(("cuts", "tile"), None),
        P("tile", None),
        P(("cuts", "tile"), None, None),
        P(("cuts", "tile"), None, None),
        P(("cuts", "tile"), None),
        P(("cuts", "tile"), None, None),
        P(("cuts", "tile"), None),
    )
    out_specs = (P(("cuts", "tile"), None, None), P(("cuts", "tile"), None, None))
    return jax.shard_map(local, mesh=mesh, in_specs=in_specs, out_specs=out_specs, check_vma=False)
```

```python
import jax
import jax.numpy as jnp
from jax import lax
from jax.experimental import pallas as pl
from jax.experimental.pallas import tpu as pltpu
from jax.sharding import PartitionSpec as P

NX = 256
NY = 256
TAPS = 4
ZDEV = 1
LOAD_ROWS = 1024
UNROLL = 8
LEVELS = 32767.0
ROUNDER = 12582912.0
WEIGHT = 0.15
GROUPS = 8
GROUP = NY // GROUPS
LANES = 128
PARTS = NX // LANES


def code(plane):
    coded, scales = [], []
    for g in range(GROUPS):
        block = plane[g * GROUP : (g + 1) * GROUP]
        most = jnp.maximum(jnp.max(jnp.abs(block), axis=0, keepdims=True), 1e-30)
        coded.append((block * (LEVELS / most) + ROUNDER - ROUNDER).astype(jnp.int32).astype(jnp.int16))
        scales.append(most * (1.0 / LEVELS))
    return jnp.concatenate(coded, axis=0), jnp.concatenate(scales, axis=0)


def decode(coded, scale):
    parts = []
    for g in range(GROUPS):
        part = coded[g * GROUP : (g + 1) * GROUP].astype(jnp.int32).astype(jnp.float32)
        parts.append(part * scale[g : g + 1])
    return jnp.concatenate(parts, axis=0)


def line_sum_kernel(
    slots_in, lines_in, counts, acquired, kept_out, sent_out,
    rows, staged, even, odd, slots, lines, load_sem, index_sem,
):
    tile = pl.program_id(0)
    loads = acquired.shape[0] // LOAD_ROWS

    def load(step):
        return pltpu.make_async_copy(
            acquired.at[pl.ds(pl.multiple_of(step * LOAD_ROWS, LOAD_ROWS), LOAD_ROWS)],
            staged.at[step],
            load_sem.at[step],
        )

    index_copies = (
        pltpu.make_async_copy(slots_in.at[0], slots, index_sem.at[0]),
        pltpu.make_async_copy(lines_in.at[0], lines, index_sem.at[1]),
    )

    @pl.when(tile == 0)
    def _():
        for copy in index_copies:
            copy.start()

        @pl.loop(0, loads)
        def _(step):
            load(step).start()

        @pl.loop(0, loads)
        def _(step):
            load(step).wait()
            block = staged[step].astype(jnp.float32)
            first = step * LOAD_ROWS * PARTS
            for part in range(PARTS):
                rows[pl.ds(first + part, LOAD_ROWS, stride=PARTS), :] = block[
                    :, part * LANES : (part + 1) * LANES
                ]

        for copy in index_copies:
            copy.wait()

    even[...] = jnp.zeros_like(even)
    odd[...] = jnp.zeros_like(odd)
    count = counts[0, tile]
    groups = count // UNROLL

    def spot(ref, j):
        return pl.ds(pl.multiple_of(ref[tile, j] * PARTS, PARTS), PARTS)

    @pl.loop(0, groups)
    def _(group):
        first = group * UNROLL
        spots = [spot(lines, first + u) for u in range(UNROLL)]
        added = [rows[spot(slots, first + u), :] for u in range(UNROLL)]
        for u in range(UNROLL):
            total = (even, odd)[u % 2]
            total[spots[u], :] += added[u]

    @pl.loop(groups * UNROLL, count)
    def _(j):
        even[spot(lines, j), :] += rows[spot(slots, j), :]

    core = lax.axis_index("cuts") % 2
    for x in range(kept_out.shape[0]):
        for out, core_to in ((kept_out, core), (sent_out, 1 - core)):
            first = (x * 2 + core_to) * NY * PARTS
            for part in range(PARTS):
                span = pl.ds(first + part, NY, stride=PARTS)
                out[x, 0, :, part * LANES : (part + 1) * LANES] = even[span, :] + odd[span, :]


def line_sums(acquired, slots, lines, counts, cut_count):
    tile_count = slots.shape[1]
    side = cut_count // 2
    rows_dev = acquired.shape[0]
    loads = rows_dev // LOAD_ROWS
    group_lines = cut_count * NY
    hbm = pl.BlockSpec(memory_space=pl.ANY)
    return pl.pallas_call(
        line_sum_kernel,
        grid=(tile_count,),
        out_shape=(
            jax.ShapeDtypeStruct((side, tile_count, NY, NX), jnp.float32),
            jax.ShapeDtypeStruct((side, tile_count, NY, NX), jnp.float32),
        ),
        in_specs=[hbm, hbm, pl.BlockSpec(memory_space=pltpu.SMEM), hbm],
        out_specs=(
            pl.BlockSpec((side, 1, NY, NX), lambda t: (0, t, 0, 0)),
            pl.BlockSpec((side, 1, NY, NX), lambda t: (0, t, 0, 0)),
        ),
        scratch_shapes=[
            pltpu.VMEM((rows_dev * PARTS, LANES), jnp.float32),
            pltpu.VMEM((loads, LOAD_ROWS, NX), jnp.bfloat16),
            pltpu.VMEM((group_lines * PARTS, LANES), jnp.float32),
            pltpu.VMEM((group_lines * PARTS, LANES), jnp.float32),
            pltpu.SMEM(slots.shape[1:], jnp.int32),
            pltpu.SMEM(lines.shape[1:], jnp.int32),
            pltpu.SemaphoreType.DMA((loads,)),
            pltpu.SemaphoreType.DMA((2,)),
        ],
        compiler_params=pltpu.CompilerParams(vmem_limit_bytes=62 * 1024 * 1024),
        name="line_sums",
    )(slots, lines, counts, acquired)


def shifted(plane, by, axis):
    zeros = jnp.zeros((abs(by), NX) if axis == 0 else (NY, abs(by)), plane.dtype)
    size = plane.shape[axis]
    if by > 0:
        return jnp.concatenate([zeros, lax.slice_in_dim(plane, 0, size - by, axis=axis)], axis)
    return jnp.concatenate([lax.slice_in_dim(plane, -by, size, axis=axis), zeros], axis)


def in_plane(plane):
    around = shifted(plane, 1, 0) + shifted(plane, -1, 0)
    around += shifted(plane, 1, 1) + shifted(plane, -1, 1)
    return (1.0 - 6.0 * WEIGHT) * plane + WEIGHT * around


def field_kernel(
    kept_sums, sent_sums, stencil, read_ids, read_counts, field_out, returned,
    own, core_in, chosen, q1_out, q1_in, s1_out, s1_in, q2_out, q2_in, s2_out, s2_in,
    q3_out, q3_in, s3_out, s3_in, q4_out, q4_in, s4_out, s4_in, back_out,
    own_sem, core_send, core_recv, send1, recv1, send2, recv2, send3, recv3,
    send4, recv4, send5, recv5,
):
    side, tiles = kept_sums.shape[:2]
    depth = tiles // side
    half = depth // 2
    spread = half * side
    cut, tile = lax.axis_index("cuts"), lax.axis_index("tile")
    x, core = cut // 2, cut % 2
    z, y = tile // side, tile % side
    me = cut * tiles + tile
    last = 2 * side * tiles - 1

    def at(x_to, y_to, z_to):
        return (x_to * 2 + core, z_to * side + y_to)

    def remote(src, dst, send, recv, device):
        return pltpu.make_async_remote_copy(
            src_ref=src, dst_ref=dst, send_sem=send, recv_sem=recv,
            device_id=device, device_id_type=pl.DeviceIdType.MESH,
        )

    partner = (x * 2 + 1 - core, tile)
    barrier = pltpu.get_barrier_semaphore()

    def greet(device):
        pl.semaphore_signal(
            barrier, inc=1, device_id=device, device_id_type=pl.DeviceIdType.MESH
        )

    greet(partner)
    for r in range(1, side):
        greet(at((x + r) % side, y, z))
    for s in range(1, tiles):
        greet((cut, (tile + s) % tiles))
    reach = (-2, -1, 1, 2)
    there = [(me + step >= 0) & (me + step <= last) for step in reach]
    for step, exists in zip(reach, there):
        @pl.when(exists)
        def _():
            greet(((me + step) // tiles, (me + step) % tiles))
    met = 1 + side - 1 + tiles - 1
    for exists in there:
        met = met + jnp.where(exists, 1, 0)
    pl.semaphore_wait(barrier, met)

    def place(r, group, i):
        h, o = i // side, i % side
        if group == 0:
            return (x + r) % side, h * side + (y + 1 + o) % side
        return (x + 1 + o) % side, (half + h) * side + (y + r) % side

    def core_copy(r, group, i):
        x_to, t_to = place(r, group, i)
        slot = (r - 1, group, i)
        return remote(
            sent_sums.at[x_to, t_to], core_in.at[slot], core_send.at[slot], core_recv.at[slot], partner
        )

    def own_copy(r, group, i):
        x_to, t_to = place(r, group, i)
        return pltpu.make_async_copy(
            kept_sums.at[x_to, t_to], own.at[r - 1, group, i], own_sem.at[r - 1, group, i]
        )

    @pl.loop(0, side * spread)
    def _(n):
        r, i = n // spread + 1, n % spread
        for group in range(2):
            core_copy(r, group, i).start()
            own_copy(r, group, i).start()

    reads = returned.shape[1]
    field_lines = lax.broadcasted_iota(jnp.int32, (NY, reads), 0)
    read_index = lax.broadcasted_iota(jnp.int32, (1, reads), 1)
    for t2 in range(tiles):
        wanted = jnp.where(read_index < read_counts[0, t2], read_ids[0, t2 : t2 + 1, :], -1)
        chosen[t2] = jnp.where(field_lines == wanted, 1.0, 0.0).astype(jnp.bfloat16)

    def pair(q_out, q_in, s_out, s_in, send, recv, at_out, at_in, device):
        return (
            remote(q_out.at[at_out], q_in.at[at_in], send.at[(0, *at_in)], recv.at[(0, *at_in)], device),
            remote(s_out.at[at_out], s_in.at[at_in], send.at[(1, *at_in)], recv.at[(1, *at_in)], device),
        )

    def copies1(r, group, i):
        device = at((x + r) % side, y, z) if group == 0 else at(x, (y + r) % side, z)
        slot = (r - 1, group, i)
        return pair(q1_out, q1_in, s1_out, s1_in, send1, recv1, slot, slot, device)

    def copies2(group, o, h):
        r = o + 1
        device = at(x, (y + r) % side, z) if group == 0 else at((x + r) % side, y, z)
        slot = (group, o, h)
        return pair(q2_out, q2_in, s2_out, s2_in, send2, recv2, slot, slot, device)

    def copies3(s):
        slot = (s - 1,)
        return pair(
            q3_out, q3_in, s3_out, s3_in, send3, recv3, slot, slot, at(x, y, (z + s) % depth)
        )

    def chip_sum(r, group, i):
        core_copy(r, group, i).wait_recv()
        own_copy(r, group, i).wait()
        return own[r - 1, group, i] + core_in[r - 1, group, i]

    @pl.loop(0, (side - 1) * spread)
    def _(n):
        r, i = n // spread + 1, n % spread
        for group in range(2):
            q1_out[r - 1, group, i], s1_out[r - 1, group, i] = code(chip_sum(r, group, i))
            for copy in copies1(r, group, i):
                copy.start()

    def kept(group, i):
        total = chip_sum(side, group, i)
        for r in range(1, side):
            for copy in copies1(r, group, i):
                copy.wait_recv()
            total += decode(q1_in[r - 1, group, i], s1_in[r - 1, group, i])
        return total

    @pl.loop(0, half)
    def _(h):
        for o in range(side - 1):
            for group in range(2):
                q2_out[group, o, h], s2_out[group, o, h] = code(kept(group, h * side + o))
                for copy in copies2(group, o, h):
                    copy.start()
        for group in range(2):
            i = h * side + side - 1
            own[side - 1, group, i] = kept(group, i)

    def column(z_to):
        group, h = z_to // half, z_to % half
        total = own[side - 1, group, h * side + side - 1]
        for o in range(side - 1):
            total += decode(q2_in[group, o, h], s2_in[group, o, h])
        return total

    def column_of(h, group):
        for o in range(side - 1):
            for copy in copies2(group, o, h):
                copy.wait_recv()
        z_to = group * half + h
        s = (z_to - z + depth) % depth

        @pl.when(s > 0)
        def _():
            q3_out[s - 1], s3_out[s - 1] = code(column(z_to))
            for copy in copies3(s):
                copy.start()

    @pl.loop(0, half)
    def _(h):
        for group in range(2):
            column_of(h, group)

    lines = column(z)
    for s in range(1, depth):
        for copy in copies3(s):
            copy.wait_recv()
        lines += decode(q3_in[s - 1], s3_in[s - 1])

    weights = stencil[...]
    raw = jnp.zeros((NY, NX), jnp.float32)
    rest = lines
    product = jnp.zeros((NY, TAPS * NX), jnp.float32)
    for _ in range(3):
        part = rest.astype(jnp.bfloat16)
        rest = rest - part.astype(jnp.float32)
        product += jnp.dot(part, weights, preferred_element_type=jnp.float32)
    raw = product[:, :NX]
    for k in range(1, TAPS):
        term = product[:, k * NX : (k + 1) * NX]
        raw += jnp.concatenate([term[NY - k :], term[: NY - k]], axis=0)

    q4_out[...], s4_out[...] = code(raw)

    def copies4(n):
        to = me + reach[n]
        device = (to // tiles, to % tiles)
        return (
            remote(q4_out, q4_in.at[n], send4.at[0, n], recv4.at[0, n], device),
            remote(s4_out, s4_in.at[n], send4.at[1, n], recv4.at[1, n], device),
        )

    for n in range(4):
        @pl.when(there[n])
        def _():
            for copy in copies4(n):
                copy.start()

    for n in range(4):
        from_there = there[3 - n]

        @pl.when(from_there)
        def _():
            for copy in copies4(n):
                copy.wait_recv()

        @pl.when(jnp.logical_not(from_there))
        def _():
            q4_in[n] = jnp.zeros((NY, NX), jnp.int16)
            s4_in[n] = jnp.zeros((GROUPS, NX), jnp.float32)

    near = decode(q4_in[1], s4_in[1]) + decode(q4_in[2], s4_in[2])
    far = decode(q4_in[0], s4_in[0]) + decode(q4_in[3], s4_in[3])
    beside = jnp.where(there[1], 1.0, 0.0) + jnp.where(there[2], 1.0, 0.0)
    once = in_plane(raw) + (2.0 * WEIGHT) * near
    smooth = in_plane(once) + (WEIGHT * WEIGHT) * (far + beside * raw)
    field = smooth.astype(jnp.bfloat16)
    field_out[0] = field

    def back(t2):
        return lax.dot_general(
            chosen[t2], field_out[0], (((0,), (0,)), ((), ())), preferred_element_type=jnp.float32
        ).astype(jnp.bfloat16)

    def copy5(s):
        return remote(
            back_out.at[s - 1], returned.at[tile], send5.at[s - 1], recv5.at[s - 1],
            (cut, (tile + s) % tiles),
        )

    @pl.loop(1, tiles)
    def _(s):
        back_out[s - 1] = back((tile + s) % tiles)
        copy5(s).start()

    returned[tile] = back(tile)

    @pl.loop(0, side * spread)
    def _(n):
        for group in range(2):
            core_copy(n // spread + 1, group, n % spread).wait_send()

    @pl.loop(0, (side - 1) * spread)
    def _(n):
        for group in range(2):
            for copy in copies1(n // spread + 1, group, n % spread):
                copy.wait_send()

    @pl.loop(0, (side - 1) * half)
    def _(i):
        for group in range(2):
            for copy in copies2(group, i // half, i % half):
                copy.wait_send()

    @pl.loop(1, depth)
    def _(s):
        for copy in copies3(s):
            copy.wait_send()

    for n in range(4):
        @pl.when(there[n])
        def _():
            for copy in copies4(n):
                copy.wait_send()

    @pl.loop(1, tiles)
    def _(s):
        copy5(s).wait_send()
        source = (tile - s + tiles) % tiles
        remote(
            back_out.at[s - 1], returned.at[source], send5.at[s - 1], recv5.at[s - 1],
            (cut, (tile + s) % tiles),
        ).wait_recv()


def finish(sums, stencil, read_ids, read_counts):
    side, tiles = sums[0].shape[:2]
    reads = read_ids.shape[2]
    depth = tiles // side
    half = depth // 2
    spread = half * side
    dma = pltpu.SemaphoreType.DMA

    def coded(*lead):
        return [
            pltpu.VMEM((*lead, NY, NX), jnp.int16),
            pltpu.VMEM((*lead, NY, NX), jnp.int16),
            pltpu.VMEM((*lead, GROUPS, NX), jnp.float32),
            pltpu.VMEM((*lead, GROUPS, NX), jnp.float32),
        ]

    vmem = pl.BlockSpec(memory_space=pltpu.VMEM)
    hbm = pl.BlockSpec(memory_space=pl.ANY)
    return pl.pallas_call(
        field_kernel,
        out_shape=(
            jax.ShapeDtypeStruct((1, NY, NX), jnp.bfloat16),
            jax.ShapeDtypeStruct((tiles, reads, NX), jnp.bfloat16),
        ),
        in_specs=[hbm, hbm, vmem, vmem, pl.BlockSpec(memory_space=pltpu.SMEM)],
        out_specs=(vmem, vmem),
        scratch_shapes=[
            pltpu.VMEM((side, 2, spread, NY, NX), jnp.float32),
            pltpu.VMEM((side, 2, spread, NY, NX), jnp.float32),
            pltpu.VMEM((tiles, NY, reads), jnp.bfloat16),
            *coded(side - 1, 2, spread),
            *coded(2, side - 1, half),
            *coded(depth - 1),
            pltpu.VMEM((NY, NX), jnp.int16),
            pltpu.VMEM((4, NY, NX), jnp.int16),
            pltpu.VMEM((GROUPS, NX), jnp.float32),
            pltpu.VMEM((4, GROUPS, NX), jnp.float32),
            pltpu.VMEM((tiles - 1, reads, NX), jnp.bfloat16),
            dma((side, 2, spread)),
            dma((side, 2, spread)),
            dma((side, 2, spread)),
            dma((2, side - 1, 2, spread)),
            dma((2, side - 1, 2, spread)),
            dma((2, 2, side - 1, half)),
            dma((2, 2, side - 1, half)),
            dma((2, depth - 1)),
            dma((2, depth - 1)),
            dma((2, 4)),
            dma((2, 4)),
            dma((tiles - 1,)),
            dma((tiles - 1,)),
        ],
        compiler_params=pltpu.CompilerParams(
            collective_id=0, has_side_effects=True, vmem_limit_bytes=62 * 1024 * 1024
        ),
        name="reduce_smooth_return",
    )(*sums, stencil, read_ids, read_counts)


def local(acquired, stencil, send_slots, send_lines, send_counts, return_slots, return_counts):
    cut_count = lax.axis_size("cuts")
    sums = line_sums(acquired, send_slots, send_lines, send_counts, cut_count)
    return finish(sums, stencil, return_slots, return_counts)


def solution(mesh):
    in_specs = (
        P(("cuts", "tile"), None),
        P("tile", None),
        P(("cuts", "tile"), None, None),
        P(("cuts", "tile"), None, None),
        P(("cuts", "tile"), None),
        P(("cuts", "tile"), None, None),
        P(("cuts", "tile"), None),
    )
    out_specs = (P(("cuts", "tile"), None, None), P(("cuts", "tile"), None, None))
    return jax.shard_map(local, mesh=mesh, in_specs=in_specs, out_specs=out_specs, check_vma=False)
```

```python
import jax
import jax.numpy as jnp
from jax import lax
from jax.experimental import pallas as pl
from jax.experimental.pallas import tpu as pltpu
from jax.sharding import PartitionSpec as P

NX = 256
NY = 256
TAPS = 4
ZDEV = 1
LOAD_ROWS = 1024
UNROLL = 8
LEVELS = 32767.0
ROUNDER = 12582912.0
WEIGHT = 0.15
GROUPS = 8
GROUP = NY // GROUPS
LANES = 128
PARTS = NX // LANES


def code(plane):
    coded, scales = [], []
    for g in range(GROUPS):
        block = plane[g * GROUP : (g + 1) * GROUP]
        most = jnp.maximum(jnp.max(jnp.abs(block), axis=0, keepdims=True), 1e-30)
        coded.append((block * (LEVELS / most) + ROUNDER - ROUNDER).astype(jnp.int32).astype(jnp.int16))
        scales.append(most * (1.0 / LEVELS))
    return jnp.concatenate(coded, axis=0), jnp.concatenate(scales, axis=0)


def decode(coded, scale):
    parts = []
    for g in range(GROUPS):
        part = coded[g * GROUP : (g + 1) * GROUP].astype(jnp.int32).astype(jnp.float32)
        parts.append(part * scale[g : g + 1])
    return jnp.concatenate(parts, axis=0)


def line_sum_kernel(
    slots_in, lines_in, counts, acquired, kept_out, sent_out,
    rows, staged, even, odd, slots, lines, load_sem, index_sem,
):
    tile = pl.program_id(0)
    loads = acquired.shape[0] // LOAD_ROWS

    def load(step):
        return pltpu.make_async_copy(
            acquired.at[pl.ds(pl.multiple_of(step * LOAD_ROWS, LOAD_ROWS), LOAD_ROWS)],
            staged.at[step],
            load_sem.at[step],
        )

    index_copies = (
        pltpu.make_async_copy(slots_in.at[0], slots, index_sem.at[0]),
        pltpu.make_async_copy(lines_in.at[0], lines, index_sem.at[1]),
    )

    @pl.when(tile == 0)
    def _():
        for copy in index_copies:
            copy.start()

        @pl.loop(0, loads)
        def _(step):
            load(step).start()

        @pl.loop(0, loads)
        def _(step):
            load(step).wait()
            block = staged[step].astype(jnp.float32)
            first = step * LOAD_ROWS * PARTS
            for part in range(PARTS):
                rows[pl.ds(first + part, LOAD_ROWS, stride=PARTS), :] = block[
                    :, part * LANES : (part + 1) * LANES
                ]

        for copy in index_copies:
            copy.wait()

    even[...] = jnp.zeros_like(even)
    odd[...] = jnp.zeros_like(odd)
    count = counts[0, tile]
    groups = count // UNROLL

    def spot(ref, j):
        return pl.ds(pl.multiple_of(ref[tile, j] * PARTS, PARTS), PARTS)

    @pl.loop(0, groups)
    def _(group):
        first = group * UNROLL
        spots = [spot(lines, first + u) for u in range(UNROLL)]
        added = [rows[spot(slots, first + u), :] for u in range(UNROLL)]
        for u in range(0, UNROLL, 2):
            first_sum = even[spots[u], :] + added[u]
            second_sum = odd[spots[u + 1], :] + added[u + 1]
            even[spots[u], :] = first_sum
            odd[spots[u + 1], :] = second_sum

    @pl.loop(groups * UNROLL, count)
    def _(j):
        even[spot(lines, j), :] += rows[spot(slots, j), :]

    core = lax.axis_index("cuts") % 2
    for x in range(kept_out.shape[0]):
        for out, core_to in ((kept_out, core), (sent_out, 1 - core)):
            first = (x * 2 + core_to) * NY * PARTS
            for part in range(PARTS):
                span = pl.ds(first + part, NY, stride=PARTS)
                out[x, 0, :, part * LANES : (part + 1) * LANES] = even[span, :] + odd[span, :]


def line_sums(acquired, slots, lines, counts, cut_count):
    tile_count = slots.shape[1]
    side = cut_count // 2
    rows_dev = acquired.shape[0]
    loads = rows_dev // LOAD_ROWS
    group_lines = cut_count * NY
    hbm = pl.BlockSpec(memory_space=pl.ANY)
    return pl.pallas_call(
        line_sum_kernel,
        grid=(tile_count,),
        out_shape=(
            jax.ShapeDtypeStruct((side, tile_count, NY, NX), jnp.float32),
            jax.ShapeDtypeStruct((side, tile_count, NY, NX), jnp.float32),
        ),
        in_specs=[hbm, hbm, pl.BlockSpec(memory_space=pltpu.SMEM), hbm],
        out_specs=(
            pl.BlockSpec((side, 1, NY, NX), lambda t: (0, t, 0, 0)),
            pl.BlockSpec((side, 1, NY, NX), lambda t: (0, t, 0, 0)),
        ),
        scratch_shapes=[
            pltpu.VMEM((rows_dev * PARTS, LANES), jnp.float32),
            pltpu.VMEM((loads, LOAD_ROWS, NX), jnp.bfloat16),
            pltpu.VMEM((group_lines * PARTS, LANES), jnp.float32),
            pltpu.VMEM((group_lines * PARTS, LANES), jnp.float32),
            pltpu.SMEM(slots.shape[1:], jnp.int32),
            pltpu.SMEM(lines.shape[1:], jnp.int32),
            pltpu.SemaphoreType.DMA((loads,)),
            pltpu.SemaphoreType.DMA((2,)),
        ],
        compiler_params=pltpu.CompilerParams(vmem_limit_bytes=62 * 1024 * 1024),
        name="line_sums",
    )(slots, lines, counts, acquired)


def shifted(plane, by, axis):
    zeros = jnp.zeros((abs(by), NX) if axis == 0 else (NY, abs(by)), plane.dtype)
    size = plane.shape[axis]
    if by > 0:
        return jnp.concatenate([zeros, lax.slice_in_dim(plane, 0, size - by, axis=axis)], axis)
    return jnp.concatenate([lax.slice_in_dim(plane, -by, size, axis=axis), zeros], axis)


def in_plane(plane):
    around = shifted(plane, 1, 0) + shifted(plane, -1, 0)
    around += shifted(plane, 1, 1) + shifted(plane, -1, 1)
    return (1.0 - 6.0 * WEIGHT) * plane + WEIGHT * around


def field_kernel(
    kept_sums, sent_sums, stencil, read_ids, read_counts, field_out, returned,
    own, core_in, chosen, q1_out, q1_in, s1_out, s1_in, q2_out, q2_in, s2_out, s2_in,
    q3_out, q3_in, s3_out, s3_in, q4_out, q4_in, s4_out, s4_in, back_out,
    own_sem, core_send, core_recv, send1, recv1, send2, recv2, send3, recv3,
    send4, recv4, send5, recv5,
):
    side, tiles = kept_sums.shape[:2]
    depth = tiles // side
    half = depth // 2
    spread = half * side
    cut, tile = lax.axis_index("cuts"), lax.axis_index("tile")
    x, core = cut // 2, cut % 2
    z, y = tile // side, tile % side
    me = cut * tiles + tile
    last = 2 * side * tiles - 1

    def at(x_to, y_to, z_to):
        return (x_to * 2 + core, z_to * side + y_to)

    def remote(src, dst, send, recv, device):
        return pltpu.make_async_remote_copy(
            src_ref=src, dst_ref=dst, send_sem=send, recv_sem=recv,
            device_id=device, device_id_type=pl.DeviceIdType.MESH,
        )

    partner = (x * 2 + 1 - core, tile)
    barrier = pltpu.get_barrier_semaphore()

    def greet(device):
        pl.semaphore_signal(
            barrier, inc=1, device_id=device, device_id_type=pl.DeviceIdType.MESH
        )

    greet(partner)
    for r in range(1, side):
        greet(at((x + r) % side, y, z))
    for s in range(1, tiles):
        greet((cut, (tile + s) % tiles))
    reach = (-2, -1, 1, 2)
    there = [(me + step >= 0) & (me + step <= last) for step in reach]
    for step, exists in zip(reach, there):
        @pl.when(exists)
        def _():
            greet(((me + step) // tiles, (me + step) % tiles))
    met = 1 + side - 1 + tiles - 1
    for exists in there:
        met = met + jnp.where(exists, 1, 0)
    pl.semaphore_wait(barrier, met)

    def place(r, group, i):
        h, o = i // side, i % side
        if group == 0:
            return (x + r) % side, h * side + (y + 1 + o) % side
        return (x + 1 + o) % side, (half + h) * side + (y + r) % side

    def core_copy(r, group, i):
        x_to, t_to = place(r, group, i)
        slot = (r - 1, group, i)
        return remote(
            sent_sums.at[x_to, t_to], core_in.at[slot], core_send.at[slot], core_recv.at[slot], partner
        )

    def own_copy(r, group, i):
        x_to, t_to = place(r, group, i)
        return pltpu.make_async_copy(
            kept_sums.at[x_to, t_to], own.at[r - 1, group, i], own_sem.at[r - 1, group, i]
        )

    def fetch(n):
        r, i = n // spread + 1, n % spread
        for group in range(2):
            core_copy(r, group, i).start()
            own_copy(r, group, i).start()

    @pl.loop(0, (side - 1) * spread)
    def _(n):
        fetch(n)

    reads = returned.shape[1]
    field_lines = lax.broadcasted_iota(jnp.int32, (NY, reads), 0)
    read_index = lax.broadcasted_iota(jnp.int32, (1, reads), 1)
    for t2 in range(tiles):
        wanted = jnp.where(read_index < read_counts[0, t2], read_ids[0, t2 : t2 + 1, :], -1)
        chosen[t2] = jnp.where(field_lines == wanted, 1.0, 0.0).astype(jnp.bfloat16)

    def pair(q_out, q_in, s_out, s_in, send, recv, at_out, at_in, device):
        return (
            remote(q_out.at[at_out], q_in.at[at_in], send.at[(0, *at_in)], recv.at[(0, *at_in)], device),
            remote(s_out.at[at_out], s_in.at[at_in], send.at[(1, *at_in)], recv.at[(1, *at_in)], device),
        )

    def copies1(r, group, i):
        device = at((x + r) % side, y, z) if group == 0 else at(x, (y + r) % side, z)
        slot = (r - 1, group, i)
        return pair(q1_out, q1_in, s1_out, s1_in, send1, recv1, slot, slot, device)

    def copies2(group, o, h):
        r = o + 1
        device = at(x, (y + r) % side, z) if group == 0 else at((x + r) % side, y, z)
        slot = (group, o, h)
        return pair(q2_out, q2_in, s2_out, s2_in, send2, recv2, slot, slot, device)

    def copies3(s):
        slot = (s - 1,)
        return pair(
            q3_out, q3_in, s3_out, s3_in, send3, recv3, slot, slot, at(x, y, (z + s) % depth)
        )

    def chip_sum(r, group, i):
        core_copy(r, group, i).wait_recv()
        own_copy(r, group, i).wait()
        return own[r - 1, group, i] + core_in[r - 1, group, i]

    def each1(h, act):
        @pl.loop(0, (side - 1) * side)
        def _(n):
            r, i = n // side + 1, h * side + n % side
            for group in range(2):
                act(r, group, i)

    def code1(r, group, i):
        q1_out[r - 1, group, i], s1_out[r - 1, group, i] = code(chip_sum(r, group, i))

    def start1(r, group, i):
        for copy in copies1(r, group, i):
            copy.start()

    def arrive1(r, group, i):
        for copy in copies1(r, group, i):
            copy.wait_recv()

    def code_start1(r, group, i):
        code1(r, group, i)
        start1(r, group, i)

    def kept(group, i):
        total = chip_sum(side, group, i)
        for r in range(1, side):
            total += decode(q1_in[r - 1, group, i], s1_in[r - 1, group, i])
        return total

    def step2(h):
        for o in range(side - 1):
            for group in range(2):
                q2_out[group, o, h], s2_out[group, o, h] = code(kept(group, h * side + o))
                for copy in copies2(group, o, h):
                    copy.start()
        for group in range(2):
            i = h * side + side - 1
            own[side - 1, group, i] = kept(group, i)

    def column(z_to):
        group, h = z_to // half, z_to % half
        total = own[side - 1, group, h * side + side - 1]
        for o in range(side - 1):
            total += decode(q2_in[group, o, h], s2_in[group, o, h])
        return total

    def column_of(h, group):
        for o in range(side - 1):
            for copy in copies2(group, o, h):
                copy.wait_recv()
        z_to = group * half + h
        s = (z_to - z + depth) % depth

        @pl.when(s > 0)
        def _():
            q3_out[s - 1], s3_out[s - 1] = code(column(z_to))
            for copy in copies3(s):
                copy.start()

    each1(0, code_start1)

    @pl.loop((side - 1) * spread, side * spread)
    def _(n):
        fetch(n)

    for h in range(half):
        if h + 1 < half:
            each1(h + 1, code1)
        each1(h, arrive1)
        if h + 1 < half:
            each1(h + 1, start1)
        step2(h)
        for group in range(2):
            column_of(h, group)

    lines = column(z)
    for s in range(1, depth):
        for copy in copies3(s):
            copy.wait_recv()
        lines += decode(q3_in[s - 1], s3_in[s - 1])

    weights = stencil[...]
    raw = jnp.zeros((NY, NX), jnp.float32)
    rest = lines
    product = jnp.zeros((NY, TAPS * NX), jnp.float32)
    for _ in range(3):
        part = rest.astype(jnp.bfloat16)
        rest = rest - part.astype(jnp.float32)
        product += jnp.dot(part, weights, preferred_element_type=jnp.float32)
    raw = product[:, :NX]
    for k in range(1, TAPS):
        term = product[:, k * NX : (k + 1) * NX]
        raw += jnp.concatenate([term[NY - k :], term[: NY - k]], axis=0)

    q4_out[...], s4_out[...] = code(raw)

    def copies4(n):
        to = me + reach[n]
        device = (to // tiles, to % tiles)
        return (
            remote(q4_out, q4_in.at[n], send4.at[0, n], recv4.at[0, n], device),
            remote(s4_out, s4_in.at[n], send4.at[1, n], recv4.at[1, n], device),
        )

    for n in range(4):
        @pl.when(there[n])
        def _():
            for copy in copies4(n):
                copy.start()

    for n in range(4):
        from_there = there[3 - n]

        @pl.when(from_there)
        def _():
            for copy in copies4(n):
                copy.wait_recv()

        @pl.when(jnp.logical_not(from_there))
        def _():
            q4_in[n] = jnp.zeros((NY, NX), jnp.int16)
            s4_in[n] = jnp.zeros((GROUPS, NX), jnp.float32)

    near = decode(q4_in[1], s4_in[1]) + decode(q4_in[2], s4_in[2])
    far = decode(q4_in[0], s4_in[0]) + decode(q4_in[3], s4_in[3])
    beside = jnp.where(there[1], 1.0, 0.0) + jnp.where(there[2], 1.0, 0.0)
    once = in_plane(raw) + (2.0 * WEIGHT) * near
    smooth = in_plane(once) + (WEIGHT * WEIGHT) * (far + beside * raw)
    field = smooth.astype(jnp.bfloat16)
    field_out[0] = field

    def back(t2):
        return lax.dot_general(
            chosen[t2], field_out[0], (((0,), (0,)), ((), ())), preferred_element_type=jnp.float32
        ).astype(jnp.bfloat16)

    def copy5(s):
        return remote(
            back_out.at[s - 1], returned.at[tile], send5.at[s - 1], recv5.at[s - 1],
            (cut, (tile + s) % tiles),
        )

    @pl.loop(1, tiles)
    def _(s):
        back_out[s - 1] = back((tile + s) % tiles)
        copy5(s).start()

    returned[tile] = back(tile)

    @pl.loop(0, side * spread)
    def _(n):
        for group in range(2):
            core_copy(n // spread + 1, group, n % spread).wait_send()

    @pl.loop(0, (side - 1) * spread)
    def _(n):
        for group in range(2):
            for copy in copies1(n // spread + 1, group, n % spread):
                copy.wait_send()

    @pl.loop(0, (side - 1) * half)
    def _(i):
        for group in range(2):
            for copy in copies2(group, i // half, i % half):
                copy.wait_send()

    @pl.loop(1, depth)
    def _(s):
        for copy in copies3(s):
            copy.wait_send()

    for n in range(4):
        @pl.when(there[n])
        def _():
            for copy in copies4(n):
                copy.wait_send()

    @pl.loop(1, tiles)
    def _(s):
        copy5(s).wait_send()
        source = (tile - s + tiles) % tiles
        remote(
            back_out.at[s - 1], returned.at[source], send5.at[s - 1], recv5.at[s - 1],
            (cut, (tile + s) % tiles),
        ).wait_recv()


def finish(sums, stencil, read_ids, read_counts):
    side, tiles = sums[0].shape[:2]
    reads = read_ids.shape[2]
    depth = tiles // side
    half = depth // 2
    spread = half * side
    dma = pltpu.SemaphoreType.DMA

    def coded(*lead):
        return [
            pltpu.VMEM((*lead, NY, NX), jnp.int16),
            pltpu.VMEM((*lead, NY, NX), jnp.int16),
            pltpu.VMEM((*lead, GROUPS, NX), jnp.float32),
            pltpu.VMEM((*lead, GROUPS, NX), jnp.float32),
        ]

    vmem = pl.BlockSpec(memory_space=pltpu.VMEM)
    hbm = pl.BlockSpec(memory_space=pl.ANY)
    return pl.pallas_call(
        field_kernel,
        out_shape=(
            jax.ShapeDtypeStruct((1, NY, NX), jnp.bfloat16),
            jax.ShapeDtypeStruct((tiles, reads, NX), jnp.bfloat16),
        ),
        in_specs=[hbm, hbm, vmem, vmem, pl.BlockSpec(memory_space=pltpu.SMEM)],
        out_specs=(vmem, vmem),
        scratch_shapes=[
            pltpu.VMEM((side, 2, spread, NY, NX), jnp.float32),
            pltpu.VMEM((side, 2, spread, NY, NX), jnp.float32),
            pltpu.VMEM((tiles, NY, reads), jnp.bfloat16),
            *coded(side - 1, 2, spread),
            *coded(2, side - 1, half),
            *coded(depth - 1),
            pltpu.VMEM((NY, NX), jnp.int16),
            pltpu.VMEM((4, NY, NX), jnp.int16),
            pltpu.VMEM((GROUPS, NX), jnp.float32),
            pltpu.VMEM((4, GROUPS, NX), jnp.float32),
            pltpu.VMEM((tiles - 1, reads, NX), jnp.bfloat16),
            dma((side, 2, spread)),
            dma((side, 2, spread)),
            dma((side, 2, spread)),
            dma((2, side - 1, 2, spread)),
            dma((2, side - 1, 2, spread)),
            dma((2, 2, side - 1, half)),
            dma((2, 2, side - 1, half)),
            dma((2, depth - 1)),
            dma((2, depth - 1)),
            dma((2, 4)),
            dma((2, 4)),
            dma((tiles - 1,)),
            dma((tiles - 1,)),
        ],
        compiler_params=pltpu.CompilerParams(
            collective_id=0, has_side_effects=True, vmem_limit_bytes=62 * 1024 * 1024
        ),
        name="reduce_smooth_return",
    )(*sums, stencil, read_ids, read_counts)


def local(acquired, stencil, send_slots, send_lines, send_counts, return_slots, return_counts):
    cut_count = lax.axis_size("cuts")
    sums = line_sums(acquired, send_slots, send_lines, send_counts, cut_count)
    return finish(sums, stencil, return_slots, return_counts)


def solution(mesh):
    in_specs = (
        P(("cuts", "tile"), None),
        P("tile", None),
        P(("cuts", "tile"), None, None),
        P(("cuts", "tile"), None, None),
        P(("cuts", "tile"), None),
        P(("cuts", "tile"), None, None),
        P(("cuts", "tile"), None),
    )
    out_specs = (P(("cuts", "tile"), None, None), P(("cuts", "tile"), None, None))
    return jax.shard_map(local, mesh=mesh, in_specs=in_specs, out_specs=out_specs, check_vma=False)
```

```python
import jax
import jax.numpy as jnp
from jax import lax
from jax.experimental import pallas as pl
from jax.experimental.pallas import tpu as pltpu
from jax.sharding import PartitionSpec as P

NX = 256
NY = 256
TAPS = 4
ZDEV = 1
LOAD_ROWS = 1024
UNROLL = 8
LEVELS = 32767.0
ROUNDER = 12582912.0
WEIGHT = 0.15
GROUPS = 8
GROUP = NY // GROUPS
LANES = 128
PARTS = NX // LANES


def code(plane):
    coded, scales = [], []
    for g in range(GROUPS):
        block = plane[g * GROUP : (g + 1) * GROUP]
        most = jnp.maximum(jnp.max(jnp.abs(block), axis=0, keepdims=True), 1e-30)
        coded.append((block * (LEVELS / most) + ROUNDER - ROUNDER).astype(jnp.int32).astype(jnp.int16))
        scales.append(most * (1.0 / LEVELS))
    return jnp.concatenate(coded, axis=0), jnp.concatenate(scales, axis=0)


def decode(coded, scale):
    parts = []
    for g in range(GROUPS):
        part = coded[g * GROUP : (g + 1) * GROUP].astype(jnp.int32).astype(jnp.float32)
        parts.append(part * scale[g : g + 1])
    return jnp.concatenate(parts, axis=0)


def line_sum_kernel(
    slots_in, lines_in, counts, acquired, kept_out, sent_out,
    rows, staged, even, odd, slots, lines, load_sem, index_sem,
):
    tile = pl.program_id(0)
    loads = acquired.shape[0] // LOAD_ROWS

    def load(step):
        return pltpu.make_async_copy(
            acquired.at[pl.ds(pl.multiple_of(step * LOAD_ROWS, LOAD_ROWS), LOAD_ROWS)],
            staged.at[step],
            load_sem.at[step],
        )

    index_copies = (
        pltpu.make_async_copy(slots_in.at[0], slots, index_sem.at[0]),
        pltpu.make_async_copy(lines_in.at[0], lines, index_sem.at[1]),
    )

    @pl.when(tile == 0)
    def _():
        for copy in index_copies:
            copy.start()

        @pl.loop(0, loads)
        def _(step):
            load(step).start()

        @pl.loop(0, loads)
        def _(step):
            load(step).wait()
            block = staged[step].astype(jnp.float32)
            first = step * LOAD_ROWS * PARTS
            for part in range(PARTS):
                rows[pl.ds(first + part, LOAD_ROWS, stride=PARTS), :] = block[
                    :, part * LANES : (part + 1) * LANES
                ]

        for copy in index_copies:
            copy.wait()

    even[...] = jnp.zeros_like(even)
    odd[...] = jnp.zeros_like(odd)
    count = counts[0, tile]
    groups = count // UNROLL

    row_at = rows.reshape(rows.shape[0] // PARTS, PARTS, LANES)
    even_at = even.reshape(even.shape[0] // PARTS, PARTS, LANES)
    odd_at = odd.reshape(odd.shape[0] // PARTS, PARTS, LANES)

    @pl.loop(0, groups)
    def _(group):
        first = group * UNROLL
        spots = [lines[tile, first + u] for u in range(UNROLL)]
        added = [row_at[slots[tile, first + u]] for u in range(UNROLL)]
        for u in range(0, UNROLL, 2):
            first_sum = even_at[spots[u]] + added[u]
            second_sum = odd_at[spots[u + 1]] + added[u + 1]
            even_at[spots[u]] = first_sum
            odd_at[spots[u + 1]] = second_sum

    @pl.loop(groups * UNROLL, count)
    def _(j):
        even_at[lines[tile, j]] += row_at[slots[tile, j]]

    core = lax.axis_index("cuts") % 2
    for x in range(kept_out.shape[0]):
        for out, core_to in ((kept_out, core), (sent_out, 1 - core)):
            first = (x * 2 + core_to) * NY * PARTS
            for part in range(PARTS):
                span = pl.ds(first + part, NY, stride=PARTS)
                out[x, 0, :, part * LANES : (part + 1) * LANES] = even[span, :] + odd[span, :]


def line_sums(acquired, slots, lines, counts, cut_count):
    tile_count = slots.shape[1]
    side = cut_count // 2
    rows_dev = acquired.shape[0]
    loads = rows_dev // LOAD_ROWS
    group_lines = cut_count * NY
    hbm = pl.BlockSpec(memory_space=pl.ANY)
    return pl.pallas_call(
        line_sum_kernel,
        grid=(tile_count,),
        out_shape=(
            jax.ShapeDtypeStruct((side, tile_count, NY, NX), jnp.float32),
            jax.ShapeDtypeStruct((side, tile_count, NY, NX), jnp.float32),
        ),
        in_specs=[hbm, hbm, pl.BlockSpec(memory_space=pltpu.SMEM), hbm],
        out_specs=(
            pl.BlockSpec((side, 1, NY, NX), lambda t: (0, t, 0, 0)),
            pl.BlockSpec((side, 1, NY, NX), lambda t: (0, t, 0, 0)),
        ),
        scratch_shapes=[
            pltpu.VMEM((rows_dev * PARTS, LANES), jnp.float32),
            pltpu.VMEM((loads, LOAD_ROWS, NX), jnp.bfloat16),
            pltpu.VMEM((group_lines * PARTS, LANES), jnp.float32),
            pltpu.VMEM((group_lines * PARTS, LANES), jnp.float32),
            pltpu.SMEM(slots.shape[1:], jnp.int32),
            pltpu.SMEM(lines.shape[1:], jnp.int32),
            pltpu.SemaphoreType.DMA((loads,)),
            pltpu.SemaphoreType.DMA((2,)),
        ],
        compiler_params=pltpu.CompilerParams(vmem_limit_bytes=62 * 1024 * 1024),
        name="line_sums",
    )(slots, lines, counts, acquired)


def shifted(plane, by, axis):
    zeros = jnp.zeros((abs(by), NX) if axis == 0 else (NY, abs(by)), plane.dtype)
    size = plane.shape[axis]
    if by > 0:
        return jnp.concatenate([zeros, lax.slice_in_dim(plane, 0, size - by, axis=axis)], axis)
    return jnp.concatenate([lax.slice_in_dim(plane, -by, size, axis=axis), zeros], axis)


def in_plane(plane):
    around = shifted(plane, 1, 0) + shifted(plane, -1, 0)
    around += shifted(plane, 1, 1) + shifted(plane, -1, 1)
    return (1.0 - 6.0 * WEIGHT) * plane + WEIGHT * around


def field_kernel(
    kept_sums, sent_sums, stencil, read_ids, read_counts, field_out, returned,
    own, core_in, chosen, q1_out, q1_in, s1_out, s1_in, q2_out, q2_in, s2_out, s2_in,
    q3_out, q3_in, s3_out, s3_in, q4_out, q4_in, s4_out, s4_in, back_out,
    own_sem, core_send, core_recv, send1, recv1, send2, recv2, send3, recv3,
    send4, recv4, send5, recv5,
):
    side, tiles = kept_sums.shape[:2]
    depth = tiles // side
    half = depth // 2
    spread = half * side
    cut, tile = lax.axis_index("cuts"), lax.axis_index("tile")
    x, core = cut // 2, cut % 2
    z, y = tile // side, tile % side
    me = cut * tiles + tile
    last = 2 * side * tiles - 1

    def at(x_to, y_to, z_to):
        return (x_to * 2 + core, z_to * side + y_to)

    def remote(src, dst, send, recv, device):
        return pltpu.make_async_remote_copy(
            src_ref=src, dst_ref=dst, send_sem=send, recv_sem=recv,
            device_id=device, device_id_type=pl.DeviceIdType.MESH,
        )

    partner = (x * 2 + 1 - core, tile)
    barrier = pltpu.get_barrier_semaphore()

    def greet(device):
        pl.semaphore_signal(
            barrier, inc=1, device_id=device, device_id_type=pl.DeviceIdType.MESH
        )

    greet(partner)
    for r in range(1, side):
        greet(at((x + r) % side, y, z))
    for s in range(1, tiles):
        greet((cut, (tile + s) % tiles))
    reach = (-2, -1, 1, 2)
    there = [(me + step >= 0) & (me + step <= last) for step in reach]
    for step, exists in zip(reach, there):
        @pl.when(exists)
        def _():
            greet(((me + step) // tiles, (me + step) % tiles))
    met = 1 + side - 1 + tiles - 1
    for exists in there:
        met = met + jnp.where(exists, 1, 0)
    pl.semaphore_wait(barrier, met)

    def place(r, group, i):
        h, o = i // side, i % side
        if group == 0:
            return (x + r) % side, h * side + (y + 1 + o) % side
        return (x + 1 + o) % side, (half + h) * side + (y + r) % side

    def core_copy(r, group, i):
        x_to, t_to = place(r, group, i)
        slot = (r - 1, group, i)
        return remote(
            sent_sums.at[x_to, t_to], core_in.at[slot], core_send.at[slot], core_recv.at[slot], partner
        )

    def own_copy(r, group, i):
        x_to, t_to = place(r, group, i)
        return pltpu.make_async_copy(
            kept_sums.at[x_to, t_to], own.at[r - 1, group, i], own_sem.at[r - 1, group, i]
        )

    @pl.loop(0, side * spread)
    def _(n):
        r, i = n // spread + 1, n % spread
        for group in range(2):
            core_copy(r, group, i).start()
            own_copy(r, group, i).start()

    reads = returned.shape[1]
    field_lines = lax.broadcasted_iota(jnp.int32, (NY, reads), 0)
    read_index = lax.broadcasted_iota(jnp.int32, (1, reads), 1)
    for t2 in range(tiles):
        wanted = jnp.where(read_index < read_counts[0, t2], read_ids[0, t2 : t2 + 1, :], -1)
        chosen[t2] = jnp.where(field_lines == wanted, 1.0, 0.0).T.astype(jnp.bfloat16)

    def pair(q_out, q_in, s_out, s_in, send, recv, at_out, at_in, device):
        return (
            remote(q_out.at[at_out], q_in.at[at_in], send.at[(0, *at_in)], recv.at[(0, *at_in)], device),
            remote(s_out.at[at_out], s_in.at[at_in], send.at[(1, *at_in)], recv.at[(1, *at_in)], device),
        )

    def copies1(r, group, i):
        device = at((x + r) % side, y, z) if group == 0 else at(x, (y + r) % side, z)
        slot = (r - 1, group, i)
        return pair(q1_out, q1_in, s1_out, s1_in, send1, recv1, slot, slot, device)

    def copies2(group, o, h):
        r = o + 1
        device = at(x, (y + r) % side, z) if group == 0 else at((x + r) % side, y, z)
        slot = (group, o, h)
        return pair(q2_out, q2_in, s2_out, s2_in, send2, recv2, slot, slot, device)

    def copies3(s):
        slot = (s - 1,)
        return pair(
            q3_out, q3_in, s3_out, s3_in, send3, recv3, slot, slot, at(x, y, (z + s) % depth)
        )

    def chip_sum(r, group, i):
        core_copy(r, group, i).wait_recv()
        own_copy(r, group, i).wait()
        return own[r - 1, group, i] + core_in[r - 1, group, i]

    @pl.loop(0, (side - 1) * spread)
    def _(n):
        r, i = n // spread + 1, n % spread
        for group in range(2):
            q1_out[r - 1, group, i], s1_out[r - 1, group, i] = code(chip_sum(r, group, i))
            for copy in copies1(r, group, i):
                copy.start()

    def kept(group, i):
        total = chip_sum(side, group, i)
        for r in range(1, side):
            for copy in copies1(r, group, i):
                copy.wait_recv()
            total += decode(q1_in[r - 1, group, i], s1_in[r - 1, group, i])
        return total

    @pl.loop(0, half)
    def _(h):
        for o in range(side - 1):
            for group in range(2):
                q2_out[group, o, h], s2_out[group, o, h] = code(kept(group, h * side + o))
                for copy in copies2(group, o, h):
                    copy.start()
        for group in range(2):
            i = h * side + side - 1
            own[side - 1, group, i] = kept(group, i)

    def column(z_to):
        group, h = z_to // half, z_to % half
        total = own[side - 1, group, h * side + side - 1]
        for o in range(side - 1):
            total += decode(q2_in[group, o, h], s2_in[group, o, h])
        return total

    def column_of(h, group):
        for o in range(side - 1):
            for copy in copies2(group, o, h):
                copy.wait_recv()
        z_to = group * half + h
        s = (z_to - z + depth) % depth

        @pl.when(s > 0)
        def _():
            q3_out[s - 1], s3_out[s - 1] = code(column(z_to))
            for copy in copies3(s):
                copy.start()

    @pl.loop(0, half)
    def _(h):
        for group in range(2):
            column_of(h, group)

    lines = column(z)
    for s in range(1, depth):
        for copy in copies3(s):
            copy.wait_recv()
        lines += decode(q3_in[s - 1], s3_in[s - 1])

    weights = stencil[...]
    raw = jnp.zeros((NY, NX), jnp.float32)
    rest = lines
    product = jnp.zeros((NY, TAPS * NX), jnp.float32)
    for _ in range(3):
        part = rest.astype(jnp.bfloat16)
        rest = rest - part.astype(jnp.float32)
        product += jnp.dot(part, weights, preferred_element_type=jnp.float32)
    raw = product[:, :NX]
    for k in range(1, TAPS):
        term = product[:, k * NX : (k + 1) * NX]
        raw += jnp.concatenate([term[NY - k :], term[: NY - k]], axis=0)

    q4_out[...], s4_out[...] = code(raw)

    def copies4(n):
        to = me + reach[n]
        device = (to // tiles, to % tiles)
        return (
            remote(q4_out, q4_in.at[n], send4.at[0, n], recv4.at[0, n], device),
            remote(s4_out, s4_in.at[n], send4.at[1, n], recv4.at[1, n], device),
        )

    for n in range(4):
        @pl.when(there[n])
        def _():
            for copy in copies4(n):
                copy.start()

    for n in range(4):
        from_there = there[3 - n]

        @pl.when(from_there)
        def _():
            for copy in copies4(n):
                copy.wait_recv()

        @pl.when(jnp.logical_not(from_there))
        def _():
            q4_in[n] = jnp.zeros((NY, NX), jnp.int16)
            s4_in[n] = jnp.zeros((GROUPS, NX), jnp.float32)

    near = decode(q4_in[1], s4_in[1]) + decode(q4_in[2], s4_in[2])
    far = decode(q4_in[0], s4_in[0]) + decode(q4_in[3], s4_in[3])
    beside = jnp.where(there[1], 1.0, 0.0) + jnp.where(there[2], 1.0, 0.0)
    once = in_plane(raw) + (2.0 * WEIGHT) * near
    smooth = in_plane(once) + (WEIGHT * WEIGHT) * (far + beside * raw)
    field = smooth.astype(jnp.bfloat16)
    field_out[0] = field

    def back(t2):
        lines_read = jnp.dot(chosen[t2], field_out[0], preferred_element_type=jnp.float32)
        return lines_read.astype(jnp.bfloat16)

    def copy5(s):
        return remote(
            back_out.at[s - 1], returned.at[tile], send5.at[s - 1], recv5.at[s - 1],
            (cut, (tile + s) % tiles),
        )

    @pl.loop(1, tiles)
    def _(s):
        back_out[s - 1] = back((tile + s) % tiles)
        copy5(s).start()

    returned[tile] = back(tile)

    @pl.loop(0, side * spread)
    def _(n):
        for group in range(2):
            core_copy(n // spread + 1, group, n % spread).wait_send()

    @pl.loop(0, (side - 1) * spread)
    def _(n):
        for group in range(2):
            for copy in copies1(n // spread + 1, group, n % spread):
                copy.wait_send()

    @pl.loop(0, (side - 1) * half)
    def _(i):
        for group in range(2):
            for copy in copies2(group, i // half, i % half):
                copy.wait_send()

    @pl.loop(1, depth)
    def _(s):
        for copy in copies3(s):
            copy.wait_send()

    for n in range(4):
        @pl.when(there[n])
        def _():
            for copy in copies4(n):
                copy.wait_send()

    @pl.loop(1, tiles)
    def _(s):
        copy5(s).wait_send()
        source = (tile - s + tiles) % tiles
        remote(
            back_out.at[s - 1], returned.at[source], send5.at[s - 1], recv5.at[s - 1],
            (cut, (tile + s) % tiles),
        ).wait_recv()


def finish(sums, stencil, read_ids, read_counts):
    side, tiles = sums[0].shape[:2]
    reads = read_ids.shape[2]
    depth = tiles // side
    half = depth // 2
    spread = half * side
    dma = pltpu.SemaphoreType.DMA

    def coded(*lead):
        return [
            pltpu.VMEM((*lead, NY, NX), jnp.int16),
            pltpu.VMEM((*lead, NY, NX), jnp.int16),
            pltpu.VMEM((*lead, GROUPS, NX), jnp.float32),
            pltpu.VMEM((*lead, GROUPS, NX), jnp.float32),
        ]

    vmem = pl.BlockSpec(memory_space=pltpu.VMEM)
    hbm = pl.BlockSpec(memory_space=pl.ANY)
    return pl.pallas_call(
        field_kernel,
        out_shape=(
            jax.ShapeDtypeStruct((1, NY, NX), jnp.bfloat16),
            jax.ShapeDtypeStruct((tiles, reads, NX), jnp.bfloat16),
        ),
        in_specs=[hbm, hbm, vmem, vmem, pl.BlockSpec(memory_space=pltpu.SMEM)],
        out_specs=(vmem, vmem),
        scratch_shapes=[
            pltpu.VMEM((side, 2, spread, NY, NX), jnp.float32),
            pltpu.VMEM((side, 2, spread, NY, NX), jnp.float32),
            pltpu.VMEM((tiles, reads, NY), jnp.bfloat16),
            *coded(side - 1, 2, spread),
            *coded(2, side - 1, half),
            *coded(depth - 1),
            pltpu.VMEM((NY, NX), jnp.int16),
            pltpu.VMEM((4, NY, NX), jnp.int16),
            pltpu.VMEM((GROUPS, NX), jnp.float32),
            pltpu.VMEM((4, GROUPS, NX), jnp.float32),
            pltpu.VMEM((tiles - 1, reads, NX), jnp.bfloat16),
            dma((side, 2, spread)),
            dma((side, 2, spread)),
            dma((side, 2, spread)),
            dma((2, side - 1, 2, spread)),
            dma((2, side - 1, 2, spread)),
            dma((2, 2, side - 1, half)),
            dma((2, 2, side - 1, half)),
            dma((2, depth - 1)),
            dma((2, depth - 1)),
            dma((2, 4)),
            dma((2, 4)),
            dma((tiles - 1,)),
            dma((tiles - 1,)),
        ],
        compiler_params=pltpu.CompilerParams(
            collective_id=0, has_side_effects=True, vmem_limit_bytes=62 * 1024 * 1024
        ),
        name="reduce_smooth_return",
    )(*sums, stencil, read_ids, read_counts)


def local(acquired, stencil, send_slots, send_lines, send_counts, return_slots, return_counts):
    cut_count = lax.axis_size("cuts")
    sums = line_sums(acquired, send_slots, send_lines, send_counts, cut_count)
    return finish(sums, stencil, return_slots, return_counts)


def solution(mesh):
    in_specs = (
        P(("cuts", "tile"), None),
        P("tile", None),
        P(("cuts", "tile"), None, None),
        P(("cuts", "tile"), None, None),
        P(("cuts", "tile"), None),
        P(("cuts", "tile"), None, None),
        P(("cuts", "tile"), None),
    )
    out_specs = (P(("cuts", "tile"), None, None), P(("cuts", "tile"), None, None))
    return jax.shard_map(local, mesh=mesh, in_specs=in_specs, out_specs=out_specs, check_vma=False)
```

```python
import jax
import jax.numpy as jnp
from jax import lax
from jax.experimental import pallas as pl
from jax.experimental.pallas import tpu as pltpu
from jax.sharding import PartitionSpec as P

NX = 256
NY = 256
TAPS = 4
ZDEV = 1
LOAD_ROWS = 1024
UNROLL = 32
SPARE = 8
LEVELS = 32767.0
ROUNDER = 12582912.0
WEIGHT = 0.15
GROUPS = 8
GROUP = NY // GROUPS
LANES = 128
PARTS = NX // LANES


def code(plane):
    coded, scales = [], []
    for g in range(GROUPS):
        block = plane[g * GROUP : (g + 1) * GROUP]
        most = jnp.maximum(jnp.max(jnp.abs(block), axis=0, keepdims=True), 1e-30)
        coded.append((block * (LEVELS / most) + ROUNDER - ROUNDER).astype(jnp.int32).astype(jnp.int16))
        scales.append(most * (1.0 / LEVELS))
    return jnp.concatenate(coded, axis=0), jnp.concatenate(scales, axis=0)


def decode(coded, scale):
    parts = []
    for g in range(GROUPS):
        part = coded[g * GROUP : (g + 1) * GROUP].astype(jnp.int32).astype(jnp.float32)
        parts.append(part * scale[g : g + 1])
    return jnp.concatenate(parts, axis=0)


def line_sum_kernel(
    slots_in, lines_in, counts, acquired, kept_out, sent_out,
    rows, staged, even, odd, slots, lines, load_sem, index_sem,
):
    tile = pl.program_id(0)
    loads = acquired.shape[0] // LOAD_ROWS

    def load(step):
        return pltpu.make_async_copy(
            acquired.at[pl.ds(pl.multiple_of(step * LOAD_ROWS, LOAD_ROWS), LOAD_ROWS)],
            staged.at[step],
            load_sem.at[step],
        )

    index_copies = (
        pltpu.make_async_copy(slots_in.at[0], slots, index_sem.at[0]),
        pltpu.make_async_copy(lines_in.at[0], lines, index_sem.at[1]),
    )

    @pl.when(tile == 0)
    def _():
        for copy in index_copies:
            copy.start()

        @pl.loop(0, loads)
        def _(step):
            load(step).start()

        @pl.loop(0, loads)
        def _(step):
            load(step).wait()
            block = staged[step].astype(jnp.float32)
            first = step * LOAD_ROWS * PARTS
            for part in range(PARTS):
                rows[pl.ds(first + part, LOAD_ROWS, stride=PARTS), :] = block[
                    :, part * LANES : (part + 1) * LANES
                ]

        for copy in index_copies:
            copy.wait()

    even[...] = jnp.zeros_like(even)
    odd[...] = jnp.zeros_like(odd)
    count = counts[0, tile]
    groups = count // UNROLL

    spare = even.shape[0] // PARTS - SPARE // PARTS

    def spot(index):
        return pl.ds(pl.multiple_of(index * PARTS, PARTS), PARTS)

    def add_group(group, masked):
        first = group * UNROLL
        to = [lines[tile, first + u] for u in range(UNROLL)]
        source = [slots[tile, first + u] for u in range(UNROLL)]
        if masked:
            to = [jnp.where(first + u < count, to[u], spare) for u in range(UNROLL)]
            source = [jnp.where(first + u < count, source[u], 0) for u in range(UNROLL)]
        added = [rows[spot(source[u]), :] for u in range(UNROLL)]
        for u in range(0, UNROLL, 2):
            first_sum = even[spot(to[u]), :] + added[u]
            second_sum = odd[spot(to[u + 1]), :] + added[u + 1]
            even[spot(to[u]), :] = first_sum
            odd[spot(to[u + 1]), :] = second_sum

    @pl.loop(0, groups)
    def _(group):
        add_group(group, False)

    @pl.when(groups * UNROLL < count)
    def _():
        add_group(groups, True)

    core = lax.axis_index("cuts") % 2
    for x in range(kept_out.shape[0]):
        for out, core_to in ((kept_out, core), (sent_out, 1 - core)):
            first = (x * 2 + core_to) * NY * PARTS
            for part in range(PARTS):
                span = pl.ds(first + part, NY, stride=PARTS)
                out[x, 0, :, part * LANES : (part + 1) * LANES] = even[span, :] + odd[span, :]


def line_sums(acquired, slots, lines, counts, cut_count):
    tile_count = slots.shape[1]
    side = cut_count // 2
    rows_dev = acquired.shape[0]
    loads = rows_dev // LOAD_ROWS
    assert slots.shape[2] % UNROLL == 0
    group_lines = cut_count * NY
    hbm = pl.BlockSpec(memory_space=pl.ANY)
    return pl.pallas_call(
        line_sum_kernel,
        grid=(tile_count,),
        out_shape=(
            jax.ShapeDtypeStruct((side, tile_count, NY, NX), jnp.float32),
            jax.ShapeDtypeStruct((side, tile_count, NY, NX), jnp.float32),
        ),
        in_specs=[hbm, hbm, pl.BlockSpec(memory_space=pltpu.SMEM), hbm],
        out_specs=(
            pl.BlockSpec((side, 1, NY, NX), lambda t: (0, t, 0, 0)),
            pl.BlockSpec((side, 1, NY, NX), lambda t: (0, t, 0, 0)),
        ),
        scratch_shapes=[
            pltpu.VMEM((rows_dev * PARTS, LANES), jnp.float32),
            pltpu.VMEM((loads, LOAD_ROWS, NX), jnp.bfloat16),
            pltpu.VMEM((group_lines * PARTS + SPARE, LANES), jnp.float32),
            pltpu.VMEM((group_lines * PARTS + SPARE, LANES), jnp.float32),
            pltpu.SMEM(slots.shape[1:], jnp.int32),
            pltpu.SMEM(lines.shape[1:], jnp.int32),
            pltpu.SemaphoreType.DMA((loads,)),
            pltpu.SemaphoreType.DMA((2,)),
        ],
        compiler_params=pltpu.CompilerParams(vmem_limit_bytes=62 * 1024 * 1024),
        name="line_sums",
    )(slots, lines, counts, acquired)


def shifted(plane, by, axis):
    zeros = jnp.zeros((abs(by), NX) if axis == 0 else (NY, abs(by)), plane.dtype)
    size = plane.shape[axis]
    if by > 0:
        return jnp.concatenate([zeros, lax.slice_in_dim(plane, 0, size - by, axis=axis)], axis)
    return jnp.concatenate([lax.slice_in_dim(plane, -by, size, axis=axis), zeros], axis)


def in_plane(plane):
    around = shifted(plane, 1, 0) + shifted(plane, -1, 0)
    around += shifted(plane, 1, 1) + shifted(plane, -1, 1)
    return (1.0 - 6.0 * WEIGHT) * plane + WEIGHT * around


def field_kernel(
    kept_sums, sent_sums, stencil, read_ids, read_counts, field_out, returned,
    own, core_in, chosen, q1_out, q1_in, s1_out, s1_in, q2_out, q2_in, s2_out, s2_in,
    q3_out, q3_in, s3_out, s3_in, q4_out, q4_in, s4_out, s4_in, back_out,
    own_sem, core_send, core_recv, send1, recv1, send2, recv2, send3, recv3,
    send4, recv4, send5, recv5,
):
    side, tiles = kept_sums.shape[:2]
    depth = tiles // side
    half = depth // 2
    spread = half * side
    cut, tile = lax.axis_index("cuts"), lax.axis_index("tile")
    x, core = cut // 2, cut % 2
    z, y = tile // side, tile % side
    me = cut * tiles + tile
    last = 2 * side * tiles - 1

    def at(x_to, y_to, z_to):
        return (x_to * 2 + core, z_to * side + y_to)

    def remote(src, dst, send, recv, device):
        return pltpu.make_async_remote_copy(
            src_ref=src, dst_ref=dst, send_sem=send, recv_sem=recv,
            device_id=device, device_id_type=pl.DeviceIdType.MESH,
        )

    partner = (x * 2 + 1 - core, tile)
    barrier = pltpu.get_barrier_semaphore()

    def greet(device):
        pl.semaphore_signal(
            barrier, inc=1, device_id=device, device_id_type=pl.DeviceIdType.MESH
        )

    greet(partner)
    for r in range(1, side):
        greet(at((x + r) % side, y, z))
    for s in range(1, tiles):
        greet((cut, (tile + s) % tiles))
    reach = (-2, -1, 1, 2)
    there = [(me + step >= 0) & (me + step <= last) for step in reach]
    for step, exists in zip(reach, there):
        @pl.when(exists)
        def _():
            greet(((me + step) // tiles, (me + step) % tiles))
    met = 1 + side - 1 + tiles - 1
    for exists in there:
        met = met + jnp.where(exists, 1, 0)
    pl.semaphore_wait(barrier, met)

    def place(r, group, i):
        h, o = i // side, i % side
        if group == 0:
            return (x + r) % side, h * side + (y + 1 + o) % side
        return (x + 1 + o) % side, (half + h) * side + (y + r) % side

    def core_copy(r, group, i):
        x_to, t_to = place(r, group, i)
        slot = (r - 1, group, i)
        return remote(
            sent_sums.at[x_to, t_to], core_in.at[slot], core_send.at[slot], core_recv.at[slot], partner
        )

    def own_copy(r, group, i):
        x_to, t_to = place(r, group, i)
        return pltpu.make_async_copy(
            kept_sums.at[x_to, t_to], own.at[r - 1, group, i], own_sem.at[r - 1, group, i]
        )

    @pl.loop(0, side * spread)
    def _(n):
        r, i = n // spread + 1, n % spread
        for group in range(2):
            core_copy(r, group, i).start()
            own_copy(r, group, i).start()

    reads = returned.shape[1]
    field_lines = lax.broadcasted_iota(jnp.int32, (NY, reads), 0)
    read_index = lax.broadcasted_iota(jnp.int32, (1, reads), 1)
    for t2 in range(tiles):
        wanted = jnp.where(read_index < read_counts[0, t2], read_ids[0, t2 : t2 + 1, :], -1)
        chosen[t2] = jnp.where(field_lines == wanted, 1.0, 0.0).astype(jnp.bfloat16)

    def pair(q_out, q_in, s_out, s_in, send, recv, at_out, at_in, device):
        return (
            remote(q_out.at[at_out], q_in.at[at_in], send.at[(0, *at_in)], recv.at[(0, *at_in)], device),
            remote(s_out.at[at_out], s_in.at[at_in], send.at[(1, *at_in)], recv.at[(1, *at_in)], device),
        )

    def copies1(r, group, i):
        device = at((x + r) % side, y, z) if group == 0 else at(x, (y + r) % side, z)
        slot = (r - 1, group, i)
        return pair(q1_out, q1_in, s1_out, s1_in, send1, recv1, slot, slot, device)

    def copies2(group, o, h):
        r = o + 1
        device = at(x, (y + r) % side, z) if group == 0 else at((x + r) % side, y, z)
        slot = (group, o, h)
        return pair(q2_out, q2_in, s2_out, s2_in, send2, recv2, slot, slot, device)

    def copies3(s):
        slot = (s - 1,)
        return pair(
            q3_out, q3_in, s3_out, s3_in, send3, recv3, slot, slot, at(x, y, (z + s) % depth)
        )

    def chip_sum(r, group, i):
        core_copy(r, group, i).wait_recv()
        own_copy(r, group, i).wait()
        return own[r - 1, group, i] + core_in[r - 1, group, i]

    @pl.loop(0, (side - 1) * spread)
    def _(n):
        r, i = n // spread + 1, n % spread
        for group in range(2):
            q1_out[r - 1, group, i], s1_out[r - 1, group, i] = code(chip_sum(r, group, i))
            for copy in copies1(r, group, i):
                copy.start()

    def kept(group, i):
        total = chip_sum(side, group, i)
        for r in range(1, side):
            for copy in copies1(r, group, i):
                copy.wait_recv()
            total += decode(q1_in[r - 1, group, i], s1_in[r - 1, group, i])
        return total

    @pl.loop(0, half)
    def _(h):
        for o in range(side - 1):
            for group in range(2):
                q2_out[group, o, h], s2_out[group, o, h] = code(kept(group, h * side + o))
                for copy in copies2(group, o, h):
                    copy.start()
        for group in range(2):
            i = h * side + side - 1
            own[side - 1, group, i] = kept(group, i)

    def column(z_to):
        group, h = z_to // half, z_to % half
        total = own[side - 1, group, h * side + side - 1]
        for o in range(side - 1):
            total += decode(q2_in[group, o, h], s2_in[group, o, h])
        return total

    def column_of(h, group):
        for o in range(side - 1):
            for copy in copies2(group, o, h):
                copy.wait_recv()
        z_to = group * half + h
        s = (z_to - z + depth) % depth

        @pl.when(s > 0)
        def _():
            q3_out[s - 1], s3_out[s - 1] = code(column(z_to))
            for copy in copies3(s):
                copy.start()

    @pl.loop(0, half)
    def _(h):
        for group in range(2):
            column_of(h, group)

    lines = column(z)
    for s in range(1, depth):
        for copy in copies3(s):
            copy.wait_recv()
        lines += decode(q3_in[s - 1], s3_in[s - 1])

    weights = stencil[...]
    raw = jnp.zeros((NY, NX), jnp.float32)
    rest = lines
    product = jnp.zeros((NY, TAPS * NX), jnp.float32)
    for _ in range(3):
        part = rest.astype(jnp.bfloat16)
        rest = rest - part.astype(jnp.float32)
        product += jnp.dot(part, weights, preferred_element_type=jnp.float32)
    raw = product[:, :NX]
    for k in range(1, TAPS):
        term = product[:, k * NX : (k + 1) * NX]
        raw += jnp.concatenate([term[NY - k :], term[: NY - k]], axis=0)

    q4_out[...], s4_out[...] = code(raw)

    def copies4(n):
        to = me + reach[n]
        device = (to // tiles, to % tiles)
        return (
            remote(q4_out, q4_in.at[n], send4.at[0, n], recv4.at[0, n], device),
            remote(s4_out, s4_in.at[n], send4.at[1, n], recv4.at[1, n], device),
        )

    for n in range(4):
        @pl.when(there[n])
        def _():
            for copy in copies4(n):
                copy.start()

    for n in range(4):
        from_there = there[3 - n]

        @pl.when(from_there)
        def _():
            for copy in copies4(n):
                copy.wait_recv()

        @pl.when(jnp.logical_not(from_there))
        def _():
            q4_in[n] = jnp.zeros((NY, NX), jnp.int16)
            s4_in[n] = jnp.zeros((GROUPS, NX), jnp.float32)

    near = decode(q4_in[1], s4_in[1]) + decode(q4_in[2], s4_in[2])
    far = decode(q4_in[0], s4_in[0]) + decode(q4_in[3], s4_in[3])
    beside = jnp.where(there[1], 1.0, 0.0) + jnp.where(there[2], 1.0, 0.0)
    once = in_plane(raw) + (2.0 * WEIGHT) * near
    smooth = in_plane(once) + (WEIGHT * WEIGHT) * (far + beside * raw)
    field = smooth.astype(jnp.bfloat16)
    field_out[0] = field

    def back(t2):
        return lax.dot_general(
            chosen[t2], field_out[0], (((0,), (0,)), ((), ())), preferred_element_type=jnp.float32
        ).astype(jnp.bfloat16)

    def copy5(s):
        return remote(
            back_out.at[s - 1], returned.at[tile], send5.at[s - 1], recv5.at[s - 1],
            (cut, (tile + s) % tiles),
        )

    @pl.loop(1, tiles)
    def _(s):
        back_out[s - 1] = back((tile + s) % tiles)
        copy5(s).start()

    returned[tile] = back(tile)

    @pl.loop(0, side * spread)
    def _(n):
        for group in range(2):
            core_copy(n // spread + 1, group, n % spread).wait_send()

    @pl.loop(0, (side - 1) * spread)
    def _(n):
        for group in range(2):
            for copy in copies1(n // spread + 1, group, n % spread):
                copy.wait_send()

    @pl.loop(0, (side - 1) * half)
    def _(i):
        for group in range(2):
            for copy in copies2(group, i // half, i % half):
                copy.wait_send()

    @pl.loop(1, depth)
    def _(s):
        for copy in copies3(s):
            copy.wait_send()

    for n in range(4):
        @pl.when(there[n])
        def _():
            for copy in copies4(n):
                copy.wait_send()

    @pl.loop(1, tiles)
    def _(s):
        copy5(s).wait_send()
        source = (tile - s + tiles) % tiles
        remote(
            back_out.at[s - 1], returned.at[source], send5.at[s - 1], recv5.at[s - 1],
            (cut, (tile + s) % tiles),
        ).wait_recv()


def finish(sums, stencil, read_ids, read_counts):
    side, tiles = sums[0].shape[:2]
    reads = read_ids.shape[2]
    depth = tiles // side
    half = depth // 2
    spread = half * side
    dma = pltpu.SemaphoreType.DMA

    def coded(*lead):
        return [
            pltpu.VMEM((*lead, NY, NX), jnp.int16),
            pltpu.VMEM((*lead, NY, NX), jnp.int16),
            pltpu.VMEM((*lead, GROUPS, NX), jnp.float32),
            pltpu.VMEM((*lead, GROUPS, NX), jnp.float32),
        ]

    vmem = pl.BlockSpec(memory_space=pltpu.VMEM)
    hbm = pl.BlockSpec(memory_space=pl.ANY)
    return pl.pallas_call(
        field_kernel,
        out_shape=(
            jax.ShapeDtypeStruct((1, NY, NX), jnp.bfloat16),
            jax.ShapeDtypeStruct((tiles, reads, NX), jnp.bfloat16),
        ),
        in_specs=[hbm, hbm, vmem, vmem, pl.BlockSpec(memory_space=pltpu.SMEM)],
        out_specs=(vmem, vmem),
        scratch_shapes=[
            pltpu.VMEM((side, 2, spread, NY, NX), jnp.float32),
            pltpu.VMEM((side, 2, spread, NY, NX), jnp.float32),
            pltpu.VMEM((tiles, NY, reads), jnp.bfloat16),
            *coded(side - 1, 2, spread),
            *coded(2, side - 1, half),
            *coded(depth - 1),
            pltpu.VMEM((NY, NX), jnp.int16),
            pltpu.VMEM((4, NY, NX), jnp.int16),
            pltpu.VMEM((GROUPS, NX), jnp.float32),
            pltpu.VMEM((4, GROUPS, NX), jnp.float32),
            pltpu.VMEM((tiles - 1, reads, NX), jnp.bfloat16),
            dma((side, 2, spread)),
            dma((side, 2, spread)),
            dma((side, 2, spread)),
            dma((2, side - 1, 2, spread)),
            dma((2, side - 1, 2, spread)),
            dma((2, 2, side - 1, half)),
            dma((2, 2, side - 1, half)),
            dma((2, depth - 1)),
            dma((2, depth - 1)),
            dma((2, 4)),
            dma((2, 4)),
            dma((tiles - 1,)),
            dma((tiles - 1,)),
        ],
        compiler_params=pltpu.CompilerParams(
            collective_id=0, has_side_effects=True, vmem_limit_bytes=62 * 1024 * 1024
        ),
        name="reduce_smooth_return",
    )(*sums, stencil, read_ids, read_counts)


def local(acquired, stencil, send_slots, send_lines, send_counts, return_slots, return_counts):
    cut_count = lax.axis_size("cuts")
    sums = line_sums(acquired, send_slots, send_lines, send_counts, cut_count)
    return finish(sums, stencil, return_slots, return_counts)


def solution(mesh):
    in_specs = (
        P(("cuts", "tile"), None),
        P("tile", None),
        P(("cuts", "tile"), None, None),
        P(("cuts", "tile"), None, None),
        P(("cuts", "tile"), None),
        P(("cuts", "tile"), None, None),
        P(("cuts", "tile"), None),
    )
    out_specs = (P(("cuts", "tile"), None, None), P(("cuts", "tile"), None, None))
    return jax.shard_map(local, mesh=mesh, in_specs=in_specs, out_specs=out_specs, check_vma=False)
```

```python
import jax
import jax.numpy as jnp
from jax import lax
from jax.experimental import pallas as pl
from jax.experimental.pallas import tpu as pltpu
from jax.sharding import PartitionSpec as P

NX = 256
NY = 256
TAPS = 4
ZDEV = 1
LOAD_ROWS = 1024
UNROLL = 8
LEVELS = 32767.0
ROUNDER = 12582912.0
WEIGHT = 0.15
GROUPS = 8
GROUP = NY // GROUPS
LANES = 128
PARTS = NX // LANES


def code(plane):
    coded, scales = [], []
    for g in range(GROUPS):
        block = plane[g * GROUP : (g + 1) * GROUP]
        most = jnp.maximum(jnp.max(jnp.abs(block), axis=0, keepdims=True), 1e-30)
        coded.append((block * (LEVELS / most) + ROUNDER - ROUNDER).astype(jnp.int32).astype(jnp.int16))
        scales.append(most * (1.0 / LEVELS))
    return jnp.concatenate(coded, axis=0), jnp.concatenate(scales, axis=0)


def decode(coded, scale):
    parts = []
    for g in range(GROUPS):
        part = coded[g * GROUP : (g + 1) * GROUP].astype(jnp.int32).astype(jnp.float32)
        parts.append(part * scale[g : g + 1])
    return jnp.concatenate(parts, axis=0)


def line_sum_kernel(
    slots_in, lines_in, counts, acquired, kept_out, sent_out,
    rows, staged, even, odd, slots, lines, load_sem, index_sem,
):
    tile = pl.program_id(0)
    loads = acquired.shape[0] // LOAD_ROWS

    def load(step):
        return pltpu.make_async_copy(
            acquired.at[pl.ds(pl.multiple_of(step * LOAD_ROWS, LOAD_ROWS), LOAD_ROWS)],
            staged.at[step],
            load_sem.at[step],
        )

    index_copies = (
        pltpu.make_async_copy(slots_in.at[0], slots, index_sem.at[0]),
        pltpu.make_async_copy(lines_in.at[0], lines, index_sem.at[1]),
    )

    @pl.when(tile == 0)
    def _():
        for copy in index_copies:
            copy.start()

        @pl.loop(0, loads)
        def _(step):
            load(step).start()

        @pl.loop(0, loads)
        def _(step):
            load(step).wait()
            block = staged[step].astype(jnp.float32)
            first = step * LOAD_ROWS * PARTS
            for part in range(PARTS):
                rows[pl.ds(first + part, LOAD_ROWS, stride=PARTS), :] = block[
                    :, part * LANES : (part + 1) * LANES
                ]

        for copy in index_copies:
            copy.wait()

    even[...] = jnp.zeros_like(even)
    odd[...] = jnp.zeros_like(odd)
    count = counts[0, tile]
    groups = count // UNROLL

    def spot(ref, j):
        return pl.ds(pl.multiple_of(ref[tile, j] * PARTS, PARTS), PARTS)

    @pl.loop(0, groups)
    def _(group):
        first = group * UNROLL
        spots = [spot(lines, first + u) for u in range(UNROLL)]
        added = [rows[spot(slots, first + u), :] for u in range(UNROLL)]
        for u in range(UNROLL):
            total = (even, odd)[u % 2]
            total[spots[u], :] += added[u]

    @pl.loop(groups * UNROLL, count)
    def _(j):
        even[spot(lines, j), :] += rows[spot(slots, j), :]

    core = lax.axis_index("cuts") % 2
    for x in range(kept_out.shape[0]):
        for out, core_to in ((kept_out, core), (sent_out, 1 - core)):
            first = (x * 2 + core_to) * NY * PARTS
            for part in range(PARTS):
                span = pl.ds(first + part, NY, stride=PARTS)
                out[x, 0, :, part * LANES : (part + 1) * LANES] = even[span, :] + odd[span, :]


def line_sums(acquired, slots, lines, counts, cut_count):
    tile_count = slots.shape[1]
    side = cut_count // 2
    rows_dev = acquired.shape[0]
    loads = rows_dev // LOAD_ROWS
    group_lines = cut_count * NY
    hbm = pl.BlockSpec(memory_space=pl.ANY)
    return pl.pallas_call(
        line_sum_kernel,
        grid=(tile_count,),
        out_shape=(
            jax.ShapeDtypeStruct((side, tile_count, NY, NX), jnp.float32),
            jax.ShapeDtypeStruct((side, tile_count, NY, NX), jnp.float32),
        ),
        in_specs=[hbm, hbm, pl.BlockSpec(memory_space=pltpu.SMEM), hbm],
        out_specs=(
            pl.BlockSpec((side, 1, NY, NX), lambda t: (0, t, 0, 0)),
            pl.BlockSpec((side, 1, NY, NX), lambda t: (0, t, 0, 0)),
        ),
        scratch_shapes=[
            pltpu.VMEM((rows_dev * PARTS, LANES), jnp.float32),
            pltpu.VMEM((loads, LOAD_ROWS, NX), jnp.bfloat16),
            pltpu.VMEM((group_lines * PARTS, LANES), jnp.float32),
            pltpu.VMEM((group_lines * PARTS, LANES), jnp.float32),
            pltpu.SMEM(slots.shape[1:], jnp.int32),
            pltpu.SMEM(lines.shape[1:], jnp.int32),
            pltpu.SemaphoreType.DMA((loads,)),
            pltpu.SemaphoreType.DMA((2,)),
        ],
        compiler_params=pltpu.CompilerParams(vmem_limit_bytes=62 * 1024 * 1024),
        name="line_sums",
    )(slots, lines, counts, acquired)


def shifted(plane, by, axis):
    zeros = jnp.zeros((abs(by), NX) if axis == 0 else (NY, abs(by)), plane.dtype)
    size = plane.shape[axis]
    if by > 0:
        return jnp.concatenate([zeros, lax.slice_in_dim(plane, 0, size - by, axis=axis)], axis)
    return jnp.concatenate([lax.slice_in_dim(plane, -by, size, axis=axis), zeros], axis)


def in_plane(plane):
    around = shifted(plane, 1, 0) + shifted(plane, -1, 0)
    around += shifted(plane, 1, 1) + shifted(plane, -1, 1)
    return (1.0 - 6.0 * WEIGHT) * plane + WEIGHT * around


def field_kernel(
    kept_sums, sent_sums, stencil, read_ids, read_counts, field_out, returned,
    own, core_in, chosen, q1_out, q1_in, s1_out, s1_in, q2_out, q2_in, s2_out, s2_in,
    q3_out, q3_in, s3_out, s3_in, q4_out, q4_in, s4_out, s4_in, back_out,
    own_sem, core_send, core_recv, send1, recv1, send2, recv2, send3, recv3,
    send4, recv4, send5, recv5,
):
    side, tiles = kept_sums.shape[:2]
    depth = tiles // side
    half = depth // 2
    spread = half * side
    cut, tile = lax.axis_index("cuts"), lax.axis_index("tile")
    x, core = cut // 2, cut % 2
    z, y = tile // side, tile % side
    me = cut * tiles + tile
    last = 2 * side * tiles - 1

    def at(x_to, y_to, z_to):
        return (x_to * 2 + core, z_to * side + y_to)

    def remote(src, dst, send, recv, device):
        return pltpu.make_async_remote_copy(
            src_ref=src, dst_ref=dst, send_sem=send, recv_sem=recv,
            device_id=device, device_id_type=pl.DeviceIdType.MESH,
        )

    partner = (x * 2 + 1 - core, tile)
    barrier = pltpu.get_barrier_semaphore()

    def greet(device):
        pl.semaphore_signal(
            barrier, inc=1, device_id=device, device_id_type=pl.DeviceIdType.MESH
        )

    greet(partner)
    for r in range(1, side):
        greet(at((x + r) % side, y, z))
    for s in range(1, tiles):
        greet((cut, (tile + s) % tiles))
    reach = (-2, -1, 1, 2)
    there = [(me + step >= 0) & (me + step <= last) for step in reach]
    for step, exists in zip(reach, there):
        @pl.when(exists)
        def _():
            greet(((me + step) // tiles, (me + step) % tiles))
    met = 1 + side - 1 + tiles - 1
    for exists in there:
        met = met + jnp.where(exists, 1, 0)
    pl.semaphore_wait(barrier, met)

    def place(r, group, i):
        h, o = i // side, i % side
        if group == 0:
            return (x + r) % side, h * side + (y + 1 + o) % side
        return (x + 1 + o) % side, (half + h) * side + (y + r) % side

    def core_copy(r, group, i):
        x_to, t_to = place(r, group, i)
        slot = (r - 1, group, i)
        return remote(
            sent_sums.at[x_to, t_to], core_in.at[slot], core_send.at[slot], core_recv.at[slot], partner
        )

    def own_copy(r, group, i):
        x_to, t_to = place(r, group, i)
        return pltpu.make_async_copy(
            kept_sums.at[x_to, t_to], own.at[r - 1, group, i], own_sem.at[r - 1, group, i]
        )

    @pl.loop(0, side * spread)
    def _(n):
        r, i = n // spread + 1, n % spread
        for group in range(2):
            core_copy(r, group, i).start()
            own_copy(r, group, i).start()

    reads = returned.shape[1]
    field_lines = lax.broadcasted_iota(jnp.int32, (NY, reads), 0)
    read_index = lax.broadcasted_iota(jnp.int32, (1, reads), 1)
    for t2 in range(tiles):
        wanted = jnp.where(read_index < read_counts[0, t2], read_ids[0, t2 : t2 + 1, :], -1)
        chosen[t2] = jnp.where(field_lines == wanted, 1.0, 0.0).astype(jnp.bfloat16)

    def pair(q_out, q_in, s_out, s_in, send, recv, at_out, at_in, device):
        return (
            remote(q_out.at[at_out], q_in.at[at_in], send.at[(0, *at_in)], recv.at[(0, *at_in)], device),
            remote(s_out.at[at_out], s_in.at[at_in], send.at[(1, *at_in)], recv.at[(1, *at_in)], device),
        )

    def copies1(r, group, i):
        device = at((x + r) % side, y, z) if group == 0 else at(x, (y + r) % side, z)
        slot = (r - 1, group, i)
        return pair(q1_out, q1_in, s1_out, s1_in, send1, recv1, slot, slot, device)

    def copies2(group, o, h):
        r = o + 1
        device = at(x, (y + r) % side, z) if group == 0 else at((x + r) % side, y, z)
        slot = (group, o, h)
        return pair(q2_out, q2_in, s2_out, s2_in, send2, recv2, slot, slot, device)

    def copies3(s):
        slot = (s - 1,)
        return pair(
            q3_out, q3_in, s3_out, s3_in, send3, recv3, slot, slot, at(x, y, (z + s) % depth)
        )

    def chip_sum(r, group, i):
        core_copy(r, group, i).wait_recv()
        own_copy(r, group, i).wait()
        return own[r - 1, group, i] + core_in[r - 1, group, i]

    @pl.loop(0, (side - 1) * spread)
    def _(n):
        r, i = n // spread + 1, n % spread
        for group in range(2):
            q1_out[r - 1, group, i], s1_out[r - 1, group, i] = code(chip_sum(r, group, i))
            for copy in copies1(r, group, i):
                copy.start()

    def kept(group, i):
        total = chip_sum(side, group, i)
        for r in range(1, side):
            for copy in copies1(r, group, i):
                copy.wait_recv()
            total += decode(q1_in[r - 1, group, i], s1_in[r - 1, group, i])
        return total

    @pl.loop(0, half)
    def _(h):
        for o in range(side - 1):
            for group in range(2):
                q2_out[group, o, h], s2_out[group, o, h] = code(kept(group, h * side + o))
                for copy in copies2(group, o, h):
                    copy.start()
        for group in range(2):
            i = h * side + side - 1
            own[side - 1, group, i] = kept(group, i)

    def column(z_to):
        group, h = z_to // half, z_to % half
        total = own[side - 1, group, h * side + side - 1]
        for o in range(side - 1):
            total += decode(q2_in[group, o, h], s2_in[group, o, h])
        return total

    def column_of(h, group):
        for o in range(side - 1):
            for copy in copies2(group, o, h):
                copy.wait_recv()
        z_to = group * half + h
        s = (z_to - z + depth) % depth

        @pl.when(s > 0)
        def _():
            q3_out[s - 1], s3_out[s - 1] = code(column(z_to))
            for copy in copies3(s):
                copy.start()

    @pl.loop(0, half)
    def _(h):
        for group in range(2):
            column_of(h, group)

    lines = column(z)
    for s in range(1, depth):
        for copy in copies3(s):
            copy.wait_recv()
        lines += decode(q3_in[s - 1], s3_in[s - 1])

    weights = stencil[...]
    raw = jnp.zeros((NY, NX), jnp.float32)
    rest = lines
    product = jnp.zeros((NY, TAPS * NX), jnp.float32)
    for _ in range(3):
        part = rest.astype(jnp.bfloat16)
        rest = rest - part.astype(jnp.float32)
        product += jnp.dot(part, weights, preferred_element_type=jnp.float32)
    raw = product[:, :NX]
    for k in range(1, TAPS):
        term = product[:, k * NX : (k + 1) * NX]
        raw += jnp.concatenate([term[NY - k :], term[: NY - k]], axis=0)

    q4_out[...], s4_out[...] = code(raw)

    def copies4(n):
        to = me + reach[n]
        device = (to // tiles, to % tiles)
        return (
            remote(q4_out, q4_in.at[n], send4.at[0, n], recv4.at[0, n], device),
            remote(s4_out, s4_in.at[n], send4.at[1, n], recv4.at[1, n], device),
        )

    for n in range(4):
        @pl.when(there[n])
        def _():
            for copy in copies4(n):
                copy.start()

    for n in range(4):
        from_there = there[3 - n]

        @pl.when(from_there)
        def _():
            for copy in copies4(n):
                copy.wait_recv()

        @pl.when(jnp.logical_not(from_there))
        def _():
            q4_in[n] = jnp.zeros((NY, NX), jnp.int16)
            s4_in[n] = jnp.zeros((GROUPS, NX), jnp.float32)

    near = decode(q4_in[1], s4_in[1]) + decode(q4_in[2], s4_in[2])
    far = decode(q4_in[0], s4_in[0]) + decode(q4_in[3], s4_in[3])
    beside = jnp.where(there[1], 1.0, 0.0) + jnp.where(there[2], 1.0, 0.0)
    once = in_plane(raw) + (2.0 * WEIGHT) * near
    smooth = in_plane(once) + (WEIGHT * WEIGHT) * (far + beside * raw)
    field_out[0] = smooth

    def back(t2):
        return lax.dot_general(
            chosen[t2], field_out[0].astype(jnp.bfloat16), (((0,), (0,)), ((), ())), preferred_element_type=jnp.float32
        ).astype(jnp.bfloat16)

    def copy5(s):
        return remote(
            back_out.at[s - 1], returned.at[tile], send5.at[s - 1], recv5.at[s - 1],
            (cut, (tile + s) % tiles),
        )

    @pl.loop(1, tiles)
    def _(s):
        back_out[s - 1] = back((tile + s) % tiles)
        copy5(s).start()

    returned[tile] = back(tile)

    @pl.loop(0, side * spread)
    def _(n):
        for group in range(2):
            core_copy(n // spread + 1, group, n % spread).wait_send()

    @pl.loop(0, (side - 1) * spread)
    def _(n):
        for group in range(2):
            for copy in copies1(n // spread + 1, group, n % spread):
                copy.wait_send()

    @pl.loop(0, (side - 1) * half)
    def _(i):
        for group in range(2):
            for copy in copies2(group, i // half, i % half):
                copy.wait_send()

    @pl.loop(1, depth)
    def _(s):
        for copy in copies3(s):
            copy.wait_send()

    for n in range(4):
        @pl.when(there[n])
        def _():
            for copy in copies4(n):
                copy.wait_send()

    @pl.loop(1, tiles)
    def _(s):
        copy5(s).wait_send()
        source = (tile - s + tiles) % tiles
        remote(
            back_out.at[s - 1], returned.at[source], send5.at[s - 1], recv5.at[s - 1],
            (cut, (tile + s) % tiles),
        ).wait_recv()


def finish(sums, stencil, read_ids, read_counts):
    side, tiles = sums[0].shape[:2]
    reads = read_ids.shape[2]
    depth = tiles // side
    half = depth // 2
    spread = half * side
    dma = pltpu.SemaphoreType.DMA

    def coded(*lead):
        return [
            pltpu.VMEM((*lead, NY, NX), jnp.int16),
            pltpu.VMEM((*lead, NY, NX), jnp.int16),
            pltpu.VMEM((*lead, GROUPS, NX), jnp.float32),
            pltpu.VMEM((*lead, GROUPS, NX), jnp.float32),
        ]

    vmem = pl.BlockSpec(memory_space=pltpu.VMEM)
    hbm = pl.BlockSpec(memory_space=pl.ANY)
    return pl.pallas_call(
        field_kernel,
        out_shape=(
            jax.ShapeDtypeStruct((1, NY, NX), jnp.float32),
            jax.ShapeDtypeStruct((tiles, reads, NX), jnp.bfloat16),
        ),
        in_specs=[hbm, hbm, vmem, vmem, pl.BlockSpec(memory_space=pltpu.SMEM)],
        out_specs=(vmem, vmem),
        scratch_shapes=[
            pltpu.VMEM((side, 2, spread, NY, NX), jnp.float32),
            pltpu.VMEM((side, 2, spread, NY, NX), jnp.float32),
            pltpu.VMEM((tiles, NY, reads), jnp.bfloat16),
            *coded(side - 1, 2, spread),
            *coded(2, side - 1, half),
            *coded(depth - 1),
            pltpu.VMEM((NY, NX), jnp.int16),
            pltpu.VMEM((4, NY, NX), jnp.int16),
            pltpu.VMEM((GROUPS, NX), jnp.float32),
            pltpu.VMEM((4, GROUPS, NX), jnp.float32),
            pltpu.VMEM((tiles - 1, reads, NX), jnp.bfloat16),
            dma((side, 2, spread)),
            dma((side, 2, spread)),
            dma((side, 2, spread)),
            dma((2, side - 1, 2, spread)),
            dma((2, side - 1, 2, spread)),
            dma((2, 2, side - 1, half)),
            dma((2, 2, side - 1, half)),
            dma((2, depth - 1)),
            dma((2, depth - 1)),
            dma((2, 4)),
            dma((2, 4)),
            dma((tiles - 1,)),
            dma((tiles - 1,)),
        ],
        compiler_params=pltpu.CompilerParams(
            collective_id=0, has_side_effects=True, vmem_limit_bytes=62 * 1024 * 1024
        ),
        name="reduce_smooth_return",
    )(*sums, stencil, read_ids, read_counts)


def local(acquired, stencil, send_slots, send_lines, send_counts, return_slots, return_counts):
    cut_count = lax.axis_size("cuts")
    sums = line_sums(acquired, send_slots, send_lines, send_counts, cut_count)
    smooth, returned = finish(sums, stencil, return_slots, return_counts)
    return smooth.astype(jnp.bfloat16), returned


def solution(mesh):
    in_specs = (
        P(("cuts", "tile"), None),
        P("tile", None),
        P(("cuts", "tile"), None, None),
        P(("cuts", "tile"), None, None),
        P(("cuts", "tile"), None),
        P(("cuts", "tile"), None, None),
        P(("cuts", "tile"), None),
    )
    out_specs = (P(("cuts", "tile"), None, None), P(("cuts", "tile"), None, None))
    return jax.shard_map(local, mesh=mesh, in_specs=in_specs, out_specs=out_specs, check_vma=False)
```
